256 devices in a mesh: band: 64 (over x, z, y_hi), grid: 4 (over y_lo, core).
Axes of the slice: x: 4, y: 4 (y_hi: 2, y_lo: 2; y = y_hi * 2 + y_lo), z: 8, core: 2. Of those that a mesh axis runs over, the one named last changes fastest.
Arguments:
- orbitals: float32 [64, 128, 128, 128], P('band', 'grid'), may hold values from -4.6 to 4.6
Outputs:
- exchange_out: float32 [64, 128, 128, 128], P('band', 'grid')
The draws below stay inside these ranges and needn't reach their ends.
All inputs are finite; a program needn't handle non-finite values.
Results may differ from the reference program's by a relative error of at most 0.0003.
Values sent between devices are 32-bit elements; how exact they have to be, the bound alone decides.
A program may use at most 128 MiB of HBM per device.

```python
import math
import jax
import jax.numpy as jnp
from jax import lax

G = 128
BANDS_DEV = 1
BLOCKS = 64
BANDS = 64


def draw_orbitals(key, part):
    key = jax.random.fold_in(key, 7)
    first_key = jax.random.fold_in(key, 0)
    shape = (BANDS, G, G, G)
    values = jax.random.normal(first_key, shape, jnp.float32)
    return jnp.clip(values, -4.6, 4.6).astype(jnp.float32)


def setup_inputs(seed: int = 0) -> dict:
    streams_of = jax.random.split(jax.random.key(seed), 2)
    return {
        "orbitals": draw_orbitals(jax.random.fold_in(streams_of[1], 71), 0),
    }


def coulomb_half(points):
    full_index = jnp.arange(points, dtype=jnp.int32)
    wrapped = jnp.minimum(full_index, points - full_index).astype(jnp.float32)
    half_index = jnp.arange(points // 2 + 1, dtype=jnp.int32).astype(jnp.float32)
    denominator = wrapped[:, None, None] ** 2 + wrapped[None, :, None] ** 2 + half_index[None, None, :] ** 2
    strength = points * math.sqrt(points) / 16.0
    return jnp.where(denominator > 0, strength / jnp.maximum(denominator, 1.0), 0.0).astype(jnp.float32)

def pair_potential(density, half_kernel):
    spectrum = jnp.fft.rfftn(density)
    return jnp.fft.irfftn(spectrum * half_kernel, s=density.shape).astype(jnp.float32)

def reference(orbitals):
    points = G
    half_kernel = coulomb_half(points)

    def one_band(band_index):
        local_orbital = lax.dynamic_index_in_dim(orbitals, band_index, 0, keepdims=False)
        block_index = band_index // BANDS_DEV
        accumulated = jnp.zeros((points, points, points), jnp.float32)
        for offset in range(-2, 3):
            first_row = ((block_index + offset) % BLOCKS * BANDS_DEV).astype(jnp.int32)
            partners = lax.dynamic_slice_in_dim(orbitals, first_row, BANDS_DEV, 0)

            def accumulate(running, partner):
                return (running + pair_potential(local_orbital * partner, half_kernel) * partner, None)
            accumulated, _ = lax.scan(accumulate, accumulated, partners)
        return -accumulated
    return lax.map(one_band, jnp.arange(BANDS, dtype=jnp.int32))
```

```python
import functools
import math

import jax
import jax.numpy as jnp
import ml_dtypes
import numpy as np
from jax import lax
from jax.experimental import pallas as pl
from jax.experimental.pallas import tpu as pltpu
from jax.sharding import PartitionSpec as P

MESH = pl.DeviceIdType.MESH
BF16 = jnp.bfloat16
F32 = jnp.float32
N = 128
Q = 32
H = 64

OH, OX, PH, PX, MH, MX, QH, QX, RH, RX = range(10)
T_OX, T_PX, T_MH, T_QH, T_MX, T_QX, T_PHA, T_PHB = range(8)
T_RX = 8
T_RH = 12
CHUNKS = 4
CH = Q // CHUNKS
T_COUNT = 16
E_OWN, E_OTHER, E_BACK = range(3)


def split(value):
    high = value.astype(BF16)
    low = (value - high.astype(F32)).astype(BF16)
    return high, low


def mm(a, b):
    return jnp.dot(a, b, preferred_element_type=F32)


def stacked(value):
    high, low = split(value)
    return jnp.concatenate([high, low], axis=0)


def kernel(x_ref, wz, wy, wx, wxi, wyi, out_ref, orb, spec, send, ga, gb, back, vt, ssem, rsem, esem, fsem, lsem):
    band = lax.axis_index("band")
    grid = lax.axis_index("grid")
    bands = lax.axis_size("band")
    core = grid % 2
    side = band % 2
    mate = (band, grid + 1 - 2 * core)
    near = (band, (grid + 2) % 4)
    cross = (band + 1 - 2 * side, (grid + 2) % 4)
    up = ((band + 2) % bands, grid)
    down = ((band + bands - 2) % bands, grid)

    own_copy = pltpu.make_async_copy(x_ref.at[0], orb.at[OH], lsem)
    own_copy.start()
    barrier = pltpu.get_barrier_semaphore()
    for other in (mate, near, cross, up, down):
        pl.semaphore_signal(barrier, inc=1, device_id=other, device_id_type=MESH)
    pl.semaphore_wait(barrier, 5)

    def transfer(index, src, dst, device):
        return pltpu.make_async_remote_copy(
            src_ref=src,
            dst_ref=dst,
            send_sem=ssem.at[index],
            recv_sem=rsem.at[index],
            device_id=device,
            device_id_type=MESH,
        )

    passed = jnp.where(side == 0, QH, MH)
    half_q = Q // 2
    moves = {
        T_OX: transfer(T_OX, x_ref.at[0], orb.at[OX], near),
        T_PX: transfer(T_PX, x_ref.at[0], orb.at[PX], cross),
        T_MH: transfer(T_MH, x_ref.at[0], orb.at[MH], up),
        T_QH: transfer(T_QH, x_ref.at[0], orb.at[QH], down),
        T_MX: transfer(T_MX, orb.at[OX], orb.at[MX], up),
        T_QX: transfer(T_QX, orb.at[OX], orb.at[QX], down),
        T_PHA: transfer(T_PHA, orb.at[PX, pl.ds(0, half_q)], orb.at[PH, pl.ds(0, half_q)], near),
        T_PHB: transfer(T_PHB, orb.at[OX, pl.ds(half_q, half_q)], orb.at[PH, pl.ds(half_q, half_q)], cross),
    }
    for k in range(CHUNKS):
        rows = pl.ds(k * CH, CH)
        moves[T_RX + k] = transfer(T_RX + k, orb.at[passed, rows], orb.at[RX, rows], cross)
        moves[T_RH + k] = transfer(T_RH + k, orb.at[RX, rows], orb.at[RH, rows], near)

    own_at = jnp.where(core == 0, 3, 1) * (Q * H)
    other_at = jnp.where(core == 0, 1, 3) * (Q * H)

    def swap(index, src, dst):
        return pltpu.make_async_remote_copy(
            src_ref=src,
            dst_ref=dst,
            send_sem=esem.at[index],
            recv_sem=fsem.at[index],
            device_id=mate,
            device_id_type=MESH,
        )

    swaps = (
        swap(E_OWN, send.at[0], spec.at[pl.ds(own_at, Q * H)]),
        swap(E_OTHER, send.at[1], spec.at[pl.ds(other_at, Q * H)]),
        swap(E_BACK, back, gb),
    )

    def forward(o_slot, j_slot, half):
        def step(i, _):
            a = i * 2
            rho = (orb[o_slot, pl.ds(a, 2)] * orb[j_slot, pl.ds(a, 2)]).reshape(2 * N, N)
            high, low = split(rho)
            t = mm(jnp.concatenate([high, low], axis=1), wz[...])
            t = t[:, :N] + t[:, N:]
            u = mm(wy[core], stacked(jnp.concatenate([t[:N], t[N:]], axis=1)))
            u = u[:N] + u[N:]
            keep = pl.multiple_of((half * 2 * Q + a) * H, 2 * H)
            spec[pl.ds(keep, 2 * H), :] = jnp.concatenate([u[:H, :N], u[:H, N:]], axis=0)
            give = pl.multiple_of(a * H, 2 * H)
            send[half, pl.ds(give, 2 * H), :] = jnp.concatenate([u[H:, :N], u[H:, N:]], axis=0)
            return 0

        lax.fori_loop(0, Q // 2, step, 0)
        swaps[half].start()

    def along_x():
        column = spec[pl.ds(0, N, stride=H), :]
        spec[pl.ds(0, N, stride=H), :] = column - jnp.where(zero_mode, jnp.mean(column, axis=0, keepdims=True), 0.0)

        def step(i, _):
            k = i * 2
            m = jnp.concatenate(
                [spec[pl.ds(k, N, stride=H), :], spec[pl.ds(k + 1, N, stride=H), :]], axis=1
            )
            s = mm(wx[...], stacked(m))
            v = jnp.concatenate(
                [vt[pl.ds(pl.multiple_of(k * N, N), N), :], vt[pl.ds(pl.multiple_of(k * N + N, N), N), :]], axis=1
            )
            s = (s[:N] + s[N:]) * v
            r = mm(wxi[core], stacked(s))
            r = r[:H] + r[H:]
            ga[pl.ds(k, Q, stride=H), :] = r[:Q, :N]
            ga[pl.ds(k + 1, Q, stride=H), :] = r[:Q, N:]
            back[pl.ds(k, Q, stride=H), :] = r[Q:, :N]
            back[pl.ds(k + 1, Q, stride=H), :] = r[Q:, N:]
            return 0

        lax.fori_loop(0, H // 2, step, 0)
        swaps[E_BACK].start()

    def inverse(j_slot, first):
        def step(i, _):
            a = i * 2
            rows = pl.ds(pl.multiple_of(a * H, 2 * H), 2 * H)
            mine, theirs = ga[rows, :], gb[rows, :]
            g = jnp.concatenate(
                [
                    jnp.concatenate([mine[:H], mine[H:]], axis=1),
                    jnp.concatenate([theirs[:H], theirs[H:]], axis=1),
                ],
                axis=0,
            )
            t = mm(wyi[core], stacked(g))
            t = t[:N] + t[N:]
            high, low = split(jnp.concatenate([t[:, :N], t[:, N:]], axis=0))
            w = mm(jnp.concatenate([high, low], axis=1), wz[...])
            w = (w[:, :N] + w[:, N:]).reshape(2, N, N) * orb[j_slot, pl.ds(a, 2)]
            if first:
                out_ref[0, pl.ds(a, 2)] = -w
            else:
                out_ref[0, pl.ds(a, 2)] -= w
            return 0

        lax.fori_loop(0, Q // 2, step, 0)

    def finish(j_slot, first=False):
        swaps[E_OWN].wait()
        swaps[E_OTHER].wait()
        along_x()
        swaps[E_BACK].wait()
        inverse(j_slot, first)

    for t in (T_OX, T_PX, T_MH, T_QH):
        moves[t].start()

    strength = N * math.sqrt(N) / 16.0 / float(N**3)
    row = lax.broadcasted_iota(jnp.int32, (N, N), 0)
    column = lax.broadcasted_iota(jnp.int32, (N, N), 1)
    row = jnp.minimum(row, N - row)
    column = jnp.minimum(column, N - column)
    plane = row * row + column * column

    zero_mode = jnp.logical_and(lax.broadcasted_iota(jnp.int32, (1, N), 1) == 0, core == 0)

    def table(i, _):
        ky = core * H + i
        ky = jnp.minimum(ky, N - ky)
        d = (plane + ky * ky).astype(F32)
        vt[pl.ds(pl.multiple_of(i * N, N), N), :] = jnp.where(d > 0, strength / jnp.maximum(d, 1.0), 0.0)
        return 0

    lax.fori_loop(0, H, table, 0)
    own_copy.wait()
    forward(OH, OH, 0)

    moves[T_OX].wait_recv()
    for t in (T_MX, T_QX, T_PHB):
        moves[t].start()
    moves[T_PX].wait_recv()
    moves[T_PHA].start()
    moves[T_MH].wait_recv()
    moves[T_QH].wait_recv()
    for k in range(CHUNKS):
        moves[T_RX + k].start()
    forward(OX, OX, 1)
    finish(OH, first=True)

    def pass_on(k):
        moves[T_RX + k].wait_recv()
        moves[T_RH + k].start()

    moves[T_PHA].wait_recv()
    forward(OX, PX, 1)
    moves[T_PHB].wait_recv()
    pass_on(0)
    forward(OH, PH, 0)
    finish(PH)
    pass_on(1)
    forward(OH, MH, 0)
    moves[T_MX].wait_recv()
    forward(OX, MX, 1)
    finish(MH)
    pass_on(2)
    forward(OH, QH, 0)
    moves[T_QX].wait_recv()
    forward(OX, QX, 1)
    pass_on(3)
    finish(QH)
    forward(OX, RX, 1)
    for k in range(CHUNKS):
        moves[T_RH + k].wait_recv()
    forward(OH, RH, 0)
    finish(RH)
    for t in range(T_COUNT):
        moves[t].wait_send()


def halves(matrix):
    high = matrix.astype(ml_dtypes.bfloat16)
    low = (matrix - high.astype(np.float64)).astype(ml_dtypes.bfloat16)
    return high, low


def left_weight(matrix):
    high, low = halves(matrix)
    return np.concatenate(
        [np.concatenate([high, high], axis=1), np.concatenate([low, np.zeros_like(low)], axis=1)], axis=0
    )


def tables():
    index = np.arange(N)
    angle = 2.0 * np.pi / N * (index[:, None] * index[None, :] % N)
    cas = np.cos(angle) + np.sin(angle)
    high, low = halves(cas)
    wz = np.concatenate(
        [np.concatenate([high, low], axis=1), np.concatenate([high, np.zeros_like(low)], axis=1)], axis=0
    )
    order = [np.concatenate([index[c * H : c * H + H], index[H - c * H : N - c * H]]) for c in (0, 1)]
    wy = np.stack([left_weight(cas[order[c]]) for c in (0, 1)])
    wyi = np.stack([left_weight(cas[:, order[c]]) for c in (0, 1)])
    wx = left_weight(cas)
    kept = [np.concatenate([index[:Q], index[Q : 2 * Q]]), np.concatenate([index[:Q], index[3 * Q :]])]
    wxi = np.stack([left_weight(cas[kept[c]]) for c in (0, 1)])
    return wz, wy, wx, wxi, wyi


def on_device(orbitals):
    weights = [jnp.asarray(w) for w in tables()]
    vmem = pl.BlockSpec(memory_space=pltpu.VMEM)
    return pl.pallas_call(
        kernel,
        out_shape=jax.ShapeDtypeStruct(orbitals.shape, F32),
        in_specs=[pl.BlockSpec(memory_space=pl.ANY)] + [vmem] * 5,
        out_specs=vmem,
        scratch_shapes=[
            pltpu.VMEM((10, Q, N, N), F32),
            pltpu.VMEM((N * H, N), F32),
            pltpu.VMEM((2, Q * H, N), F32),
            pltpu.VMEM((Q * H, N), F32),
            pltpu.VMEM((Q * H, N), F32),
            pltpu.VMEM((Q * H, N), F32),
            pltpu.VMEM((H * N, N), F32),
            pltpu.SemaphoreType.DMA((T_COUNT,)),
            pltpu.SemaphoreType.DMA((T_COUNT,)),
            pltpu.SemaphoreType.DMA((3,)),
            pltpu.SemaphoreType.DMA((3,)),
            pltpu.SemaphoreType.DMA,
        ],
        compiler_params=pltpu.CompilerParams(
            collective_id=0, has_side_effects=True, vmem_limit_bytes=56 * 1024 * 1024
        ),
    )(orbitals, *weights)


def solution(mesh):
    spec = P("band", "grid", None, None)
    return jax.shard_map(on_device, mesh=mesh, in_specs=(spec,), out_specs=spec, check_vma=False)
```

```python
import functools
import math

import jax
import jax.numpy as jnp
import ml_dtypes
import numpy as np
from jax import lax
from jax.experimental import pallas as pl
from jax.experimental.pallas import tpu as pltpu
from jax.sharding import PartitionSpec as P

MESH = pl.DeviceIdType.MESH
BF16 = jnp.bfloat16
F32 = jnp.float32
N = 128
Q = 32
H = 64

OH, OX, PH, PX, MH, MX, QH, QX, RH, RX = range(10)
T_OX, T_PX, T_MH, T_QH, T_MX, T_QX, T_PHA, T_PHB = range(8)
T_RX = 8
T_RH = 12
CHUNKS = 4
UNROLL = 4
CH = Q // CHUNKS
T_COUNT = 16
E_OWN, E_OTHER, E_BACK = range(3)


def split(value):
    high = value.astype(BF16)
    low = (value - high.astype(F32)).astype(BF16)
    return high, low


def mm(a, b):
    return jnp.dot(a, b, preferred_element_type=F32)


def stacked(value):
    high, low = split(value)
    return jnp.concatenate([high, low], axis=0)


def kernel(x_ref, wz, wy, wx, wxi, wyi, out_ref, orb, spec, send, ga, gb, back, vt, ssem, rsem, esem, fsem, lsem):
    band = lax.axis_index("band")
    grid = lax.axis_index("grid")
    bands = lax.axis_size("band")
    core = grid % 2
    side = band % 2
    mate = (band, grid + 1 - 2 * core)
    near = (band, (grid + 2) % 4)
    cross = (band + 1 - 2 * side, (grid + 2) % 4)
    up = ((band + 2) % bands, grid)
    down = ((band + bands - 2) % bands, grid)

    own_copy = pltpu.make_async_copy(x_ref.at[0], orb.at[OH], lsem)
    own_copy.start()
    barrier = pltpu.get_barrier_semaphore()
    for other in (mate, near, cross, up, down):
        pl.semaphore_signal(barrier, inc=1, device_id=other, device_id_type=MESH)
    pl.semaphore_wait(barrier, 5)

    def transfer(index, src, dst, device):
        return pltpu.make_async_remote_copy(
            src_ref=src,
            dst_ref=dst,
            send_sem=ssem.at[index],
            recv_sem=rsem.at[index],
            device_id=device,
            device_id_type=MESH,
        )

    passed = jnp.where(side == 0, QH, MH)
    half_q = Q // 2
    moves = {
        T_OX: transfer(T_OX, x_ref.at[0], orb.at[OX], near),
        T_PX: transfer(T_PX, x_ref.at[0], orb.at[PX], cross),
        T_MH: transfer(T_MH, x_ref.at[0], orb.at[MH], up),
        T_QH: transfer(T_QH, x_ref.at[0], orb.at[QH], down),
        T_MX: transfer(T_MX, orb.at[OX], orb.at[MX], up),
        T_QX: transfer(T_QX, orb.at[OX], orb.at[QX], down),
        T_PHA: transfer(T_PHA, orb.at[PX, pl.ds(0, half_q)], orb.at[PH, pl.ds(0, half_q)], near),
        T_PHB: transfer(T_PHB, orb.at[OX, pl.ds(half_q, half_q)], orb.at[PH, pl.ds(half_q, half_q)], cross),
    }
    for k in range(CHUNKS):
        rows = pl.ds(k * CH, CH)
        moves[T_RX + k] = transfer(T_RX + k, orb.at[passed, rows], orb.at[RX, rows], cross)
        moves[T_RH + k] = transfer(T_RH + k, orb.at[RX, rows], orb.at[RH, rows], near)

    own_at = jnp.where(core == 0, 3, 1) * (Q * H)
    other_at = jnp.where(core == 0, 1, 3) * (Q * H)

    def swap(index, src, dst):
        return pltpu.make_async_remote_copy(
            src_ref=src,
            dst_ref=dst,
            send_sem=esem.at[index],
            recv_sem=fsem.at[index],
            device_id=mate,
            device_id_type=MESH,
        )

    swaps = (
        swap(E_OWN, send.at[0], spec.at[pl.ds(own_at, Q * H)]),
        swap(E_OTHER, send.at[1], spec.at[pl.ds(other_at, Q * H)]),
        swap(E_BACK, back, gb),
    )

    def forward(o_slot, j_slot, half):
        def step(i, _):
            a = i * 2
            rho = (orb[o_slot, pl.ds(a, 2)] * orb[j_slot, pl.ds(a, 2)]).reshape(2 * N, N)
            high, low = split(rho)
            t = mm(jnp.concatenate([high, low], axis=1), wz[...])
            t = t[:, :N] + t[:, N:]
            u = mm(wy[core], stacked(jnp.concatenate([t[:N], t[N:]], axis=1)))
            u = u[:N] + u[N:]
            for b in range(2):
                plane = u[:, b * N : b * N + N]
                spec[pl.ds(half * 2 * Q * H + a + b, H, stride=Q), :] = plane[:H]
                send[half, pl.ds(a + b, H, stride=Q), :] = plane[H:]
            return 0

        lax.fori_loop(0, Q // 2, step, 0, unroll=UNROLL)
        swaps[half].start()

    def row_of(k):
        return jnp.concatenate(
            [spec[pl.ds(pl.multiple_of(p * Q * H + k * Q, Q), Q), :] for p in range(4)], axis=0
        )

    def along_x():
        column = row_of(0)
        column = column - jnp.where(zero_mode, jnp.mean(column, axis=0, keepdims=True), 0.0)
        for p in range(4):
            spec[pl.ds(p * Q * H, Q), :] = column[p * Q : p * Q + Q]

        def step(i, _):
            k = i * 2
            m = jnp.concatenate([row_of(k), row_of(k + 1)], axis=1)
            s = mm(wx[...], stacked(m))
            v = jnp.concatenate(
                [vt[pl.ds(pl.multiple_of(k * N, N), N), :], vt[pl.ds(pl.multiple_of(k * N + N, N), N), :]], axis=1
            )
            s = (s[:N] + s[N:]) * v
            r = mm(wxi[core], stacked(s))
            r = r[:H] + r[H:]
            ga[pl.ds(k, Q, stride=H), :] = r[:Q, :N]
            ga[pl.ds(k + 1, Q, stride=H), :] = r[:Q, N:]
            back[pl.ds(k, Q, stride=H), :] = r[Q:, :N]
            back[pl.ds(k + 1, Q, stride=H), :] = r[Q:, N:]
            return 0

        lax.fori_loop(0, H // 2, step, 0, unroll=UNROLL)
        swaps[E_BACK].start()

    def inverse(j_slot, first):
        def step(i, _):
            a = i * 2
            rows = pl.ds(pl.multiple_of(a * H, 2 * H), 2 * H)
            mine, theirs = ga[rows, :], gb[rows, :]
            g = jnp.concatenate(
                [
                    jnp.concatenate([mine[:H], mine[H:]], axis=1),
                    jnp.concatenate([theirs[:H], theirs[H:]], axis=1),
                ],
                axis=0,
            )
            t = mm(wyi[core], stacked(g))
            t = t[:N] + t[N:]
            high, low = split(jnp.concatenate([t[:, :N], t[:, N:]], axis=0))
            w = mm(jnp.concatenate([high, low], axis=1), wz[...])
            w = (w[:, :N] + w[:, N:]).reshape(2, N, N) * orb[j_slot, pl.ds(a, 2)]
            if first:
                out_ref[0, pl.ds(a, 2)] = -w
            else:
                out_ref[0, pl.ds(a, 2)] -= w
            return 0

        lax.fori_loop(0, Q // 2, step, 0, unroll=UNROLL)

    def finish(j_slot, first=False):
        swaps[E_OWN].wait()
        swaps[E_OTHER].wait()
        along_x()
        swaps[E_BACK].wait()
        inverse(j_slot, first)

    for t in (T_OX, T_PX, T_MH, T_QH):
        moves[t].start()

    strength = N * math.sqrt(N) / 16.0 / float(N**3)
    row = lax.broadcasted_iota(jnp.int32, (N, N), 0)
    column = lax.broadcasted_iota(jnp.int32, (N, N), 1)
    row = jnp.minimum(row, N - row)
    column = jnp.minimum(column, N - column)
    plane = row * row + column * column

    zero_mode = jnp.logical_and(lax.broadcasted_iota(jnp.int32, (1, N), 1) == 0, core == 0)

    def table(i, _):
        ky = core * H + i
        ky = jnp.minimum(ky, N - ky)
        d = (plane + ky * ky).astype(F32)
        vt[pl.ds(pl.multiple_of(i * N, N), N), :] = jnp.where(d > 0, strength / jnp.maximum(d, 1.0), 0.0)
        return 0

    lax.fori_loop(0, H, table, 0)
    own_copy.wait()
    forward(OH, OH, 0)

    moves[T_OX].wait_recv()
    for t in (T_MX, T_QX, T_PHB):
        moves[t].start()
    moves[T_PX].wait_recv()
    moves[T_PHA].start()
    moves[T_MH].wait_recv()
    moves[T_QH].wait_recv()
    for k in range(CHUNKS):
        moves[T_RX + k].start()
    forward(OX, OX, 1)
    finish(OH, first=True)

    def pass_on(k):
        moves[T_RX + k].wait_recv()
        moves[T_RH + k].start()

    moves[T_PHA].wait_recv()
    forward(OX, PX, 1)
    moves[T_PHB].wait_recv()
    pass_on(0)
    forward(OH, PH, 0)
    finish(PH)
    pass_on(1)
    forward(OH, MH, 0)
    moves[T_MX].wait_recv()
    forward(OX, MX, 1)
    finish(MH)
    pass_on(2)
    forward(OH, QH, 0)
    moves[T_QX].wait_recv()
    forward(OX, QX, 1)
    pass_on(3)
    finish(QH)
    forward(OX, RX, 1)
    for k in range(CHUNKS):
        moves[T_RH + k].wait_recv()
    forward(OH, RH, 0)
    finish(RH)
    for t in range(T_COUNT):
        moves[t].wait_send()


def halves(matrix):
    high = matrix.astype(ml_dtypes.bfloat16)
    low = (matrix - high.astype(np.float64)).astype(ml_dtypes.bfloat16)
    return high, low


def left_weight(matrix):
    high, low = halves(matrix)
    return np.concatenate(
        [np.concatenate([high, high], axis=1), np.concatenate([low, np.zeros_like(low)], axis=1)], axis=0
    )


def tables():
    index = np.arange(N)
    angle = 2.0 * np.pi / N * (index[:, None] * index[None, :] % N)
    cas = np.cos(angle) + np.sin(angle)
    high, low = halves(cas)
    wz = np.concatenate(
        [np.concatenate([high, low], axis=1), np.concatenate([high, np.zeros_like(low)], axis=1)], axis=0
    )
    order = [np.concatenate([index[c * H : c * H + H], index[H - c * H : N - c * H]]) for c in (0, 1)]
    wy = np.stack([left_weight(cas[order[c]]) for c in (0, 1)])
    wyi = np.stack([left_weight(cas[:, order[c]]) for c in (0, 1)])
    wx = left_weight(cas)
    kept = [np.concatenate([index[:Q], index[Q : 2 * Q]]), np.concatenate([index[:Q], index[3 * Q :]])]
    wxi = np.stack([left_weight(cas[kept[c]]) for c in (0, 1)])
    return wz, wy, wx, wxi, wyi


def on_device(orbitals):
    weights = [jnp.asarray(w) for w in tables()]
    vmem = pl.BlockSpec(memory_space=pltpu.VMEM)
    return pl.pallas_call(
        kernel,
        out_shape=jax.ShapeDtypeStruct(orbitals.shape, F32),
        in_specs=[pl.BlockSpec(memory_space=pl.ANY)] + [vmem] * 5,
        out_specs=vmem,
        scratch_shapes=[
            pltpu.VMEM((10, Q, N, N), F32),
            pltpu.VMEM((N * H, N), F32),
            pltpu.VMEM((2, Q * H, N), F32),
            pltpu.VMEM((Q * H, N), F32),
            pltpu.VMEM((Q * H, N), F32),
            pltpu.VMEM((Q * H, N), F32),
            pltpu.VMEM((H * N, N), F32),
            pltpu.SemaphoreType.DMA((T_COUNT,)),
            pltpu.SemaphoreType.DMA((T_COUNT,)),
            pltpu.SemaphoreType.DMA((3,)),
            pltpu.SemaphoreType.DMA((3,)),
            pltpu.SemaphoreType.DMA,
        ],
        compiler_params=pltpu.CompilerParams(
            collective_id=0, has_side_effects=True, vmem_limit_bytes=56 * 1024 * 1024
        ),
    )(orbitals, *weights)


def solution(mesh):
    spec = P("band", "grid", None, None)
    return jax.shard_map(on_device, mesh=mesh, in_specs=(spec,), out_specs=spec, check_vma=False)
```

```python
import functools
import math

import jax
import jax.numpy as jnp
import ml_dtypes
import numpy as np
from jax import lax
from jax.experimental import pallas as pl
from jax.experimental.pallas import tpu as pltpu
from jax.sharding import PartitionSpec as P

MESH = pl.DeviceIdType.MESH
BF16 = jnp.bfloat16
F32 = jnp.float32
N = 128
Q = 32
H = 64

OH, OX, PH, PX, MH, MX, QH, QX, RH, RX = range(10)
PART = 16
CH = 4
CHUNKS = 7
ZROWS = CHUNKS * CH
T_OX, T_PX, T_MH, T_QH, T_MXA, T_MXB, T_QXA, T_QXB, T_PHA, T_PHB, T_RXZ, T_RHZ = range(12)
T_RX = 12
T_RH = T_RX + CHUNKS
T_COUNT = T_RH + CHUNKS
SETS = 3
UNROLL = 8


def split(value):
    high = value.astype(BF16)
    low = (value - high.astype(F32)).astype(BF16)
    return high, low


def mm(a, b):
    return jnp.dot(a, b, preferred_element_type=F32)


def stacked(value):
    high, low = split(value)
    return jnp.concatenate([high, low], axis=0)


def kernel(x_ref, wz, wy, wx, wxi, wyi, out_ref, orb, spec, send, ga, gb, back, vt, ssem, rsem, esem, fsem, bsem, csem, lsem):
    band = lax.axis_index("band")
    grid = lax.axis_index("grid")
    bands = lax.axis_size("band")
    core = grid % 2
    side = band % 2
    mate = (band, grid + 1 - 2 * core)
    near = (band, (grid + 2) % 4)
    cross = (band + 1 - 2 * side, (grid + 2) % 4)
    up = ((band + 2) % bands, grid)
    down = ((band + bands - 2) % bands, grid)
    beyond = (jnp.where(side == 0, up[0], down[0]), grid)

    own_copy = pltpu.make_async_copy(x_ref.at[0], orb.at[OH], lsem)
    own_copy.start()
    barrier = pltpu.get_barrier_semaphore()
    for other in (mate, near, cross, up, down):
        pl.semaphore_signal(barrier, inc=1, device_id=other, device_id_type=MESH)
    pl.semaphore_wait(barrier, 5)

    def remote(src, dst, send_sem, recv_sem, device):
        return pltpu.make_async_remote_copy(
            src_ref=src, dst_ref=dst, send_sem=send_sem, recv_sem=recv_sem, device_id=device, device_id_type=MESH
        )

    moves = {}

    def transfer(index, src, dst, device):
        moves[index] = remote(src, dst, ssem.at[index], rsem.at[index], device)

    def passed_on(index, src_slot, dst_slot, first, count, device):
        rows = pl.ds(first, count)
        transfer(index, orb.at[src_slot, rows], orb.at[dst_slot, rows], device)

    transfer(T_OX, x_ref.at[0], orb.at[OX], near)
    transfer(T_PX, x_ref.at[0], orb.at[PX], cross)
    transfer(T_MH, x_ref.at[0], orb.at[MH], up)
    transfer(T_QH, x_ref.at[0], orb.at[QH], down)
    passed_on(T_MXA, OX, MX, 0, PART, up)
    passed_on(T_MXB, OX, MX, PART, PART, up)
    passed_on(T_QXA, OX, QX, 0, PART, down)
    passed_on(T_QXB, OX, QX, PART, PART, down)
    passed_on(T_PHA, PX, PH, 0, PART, near)
    passed_on(T_PHB, OX, PH, PART, PART, cross)
    passed_on(T_RXZ, PX, RX, ZROWS, Q - ZROWS, beyond)
    passed_on(T_RHZ, PH, RH, ZROWS, Q - ZROWS, beyond)
    far_source = jnp.where(side == 0, QH, MH)
    for k in range(CHUNKS):
        passed_on(T_RX + k, far_source, RX, k * CH, CH, cross)
        passed_on(T_RH + k, RX, RH, k * CH, CH, near)

    block = H * PART
    first_mate = jnp.where(core == 0, 6, 2) * block
    second_mate = jnp.where(core == 0, 2, 6) * block

    def swap(s, part):
        at = (first_mate if part < 2 else second_mate) + (part % 2) * block
        sem = s * 4 + part
        return remote(send.at[s, part], spec.at[s, pl.ds(at, block)], esem.at[sem], fsem.at[sem], mate)

    swaps = {(s, part): swap(s, part) for s in range(SETS) for part in range(4)}
    backs = {
        (turn, c): remote(
            back.at[c], gb.at[turn, c], bsem.at[turn * 2 + c], csem.at[turn * 2 + c], mate
        )
        for turn in range(2)
        for c in range(2)
    }

    def forward(s, o_slot, j_slot, part):
        first = (part % 2) * PART
        keep = (part % 2 + part // 2 * 4) * block

        def step(i, _):
            a = i * 2
            rho = (orb[o_slot, pl.ds(first + a, 2)] * orb[j_slot, pl.ds(first + a, 2)]).reshape(2 * N, N)
            high, low = split(rho)
            t = mm(jnp.concatenate([high, low], axis=1), wz[...])
            t = t[:, :N] + t[:, N:]
            u = mm(wy[core], stacked(jnp.concatenate([t[:N], t[N:]], axis=1)))
            u = u[:N] + u[N:]
            for b in range(2):
                plane = u[:, b * N : b * N + N]
                spec[s, pl.ds(keep + a + b, H, stride=PART), :] = plane[:H]
                send[s, part, pl.ds(a + b, H, stride=PART), :] = plane[H:]
            return 0

        lax.fori_loop(0, PART // 2, step, 0, unroll=UNROLL)
        swaps[s, part].start()

    def row_of(s, k):
        return jnp.concatenate(
            [spec[s, pl.ds(pl.multiple_of(p * block + k * PART, PART), PART), :] for p in range(8)], axis=0
        )

    def along_x(s, turn, c):
        if c == 0:
            column = row_of(s, 0)
            column = column - jnp.where(zero_mode, jnp.mean(column, axis=0, keepdims=True), 0.0)
            for p in range(8):
                spec[s, pl.ds(p * block, PART), :] = column[p * PART : p * PART + PART]

        def step(i, _):
            k = c * (H // 2) + i * 2
            m = jnp.concatenate([row_of(s, k), row_of(s, k + 1)], axis=1)
            f = mm(wx[...], stacked(m))
            v = jnp.concatenate(
                [vt[pl.ds(pl.multiple_of(k * N, N), N), :], vt[pl.ds(pl.multiple_of(k * N + N, N), N), :]], axis=1
            )
            f = (f[:N] + f[N:]) * v
            r = mm(wxi[core], stacked(f))
            r = r[:H] + r[H:]
            for b in range(2):
                plane = r[:, b * N : b * N + N]
                ga[c, pl.ds(i * 2 + b, Q, stride=H // 2), :] = plane[:Q]
                back[c, pl.ds(i * 2 + b, Q, stride=H // 2), :] = plane[Q:]
            return 0

        lax.fori_loop(0, H // 4, step, 0, unroll=UNROLL)
        backs[turn, c].start()

    def inverse(j_slot, turn, first):
        def step(i, _):
            a = i * 2
            planes = []
            for b in range(2):
                rows = pl.ds(pl.multiple_of((a + b) * (H // 2), H // 2), H // 2)
                planes.append(
                    jnp.concatenate([ga[0, rows, :], ga[1, rows, :], gb[turn, 0, rows, :], gb[turn, 1, rows, :]], axis=0)
                )
            t = mm(wyi[core], stacked(jnp.concatenate(planes, axis=1)))
            t = t[:N] + t[N:]
            high, low = split(jnp.concatenate([t[:, :N], t[:, N:]], axis=0))
            w = mm(jnp.concatenate([high, low], axis=1), wz[...])
            w = (w[:, :N] + w[:, N:]).reshape(2, N, N) * orb[j_slot, pl.ds(a, 2)]
            if first:
                out_ref[0, pl.ds(a, 2)] = -w
            else:
                out_ref[0, pl.ds(a, 2)] -= w
            return 0

        lax.fori_loop(0, Q // 2, step, 0, unroll=UNROLL)

    def finish(s, j_slot, turn, between=lambda: None, first=False):
        for part in (2, 3, 0, 1):
            swaps[s, part].wait()
        along_x(s, turn, 0)
        along_x(s, turn, 1)
        between()
        backs[turn, 0].wait()
        backs[turn, 1].wait()
        inverse(j_slot, turn, first)

    def arrived(*indices):
        for t in indices:
            moves[t].wait_recv()

    def start(*indices):
        for t in indices:
            moves[t].start()

    def pass_on(k):
        arrived(T_RX + k)
        start(T_RH + k)

    start(T_OX, T_PX, T_MH, T_QH)

    strength = N * math.sqrt(N) / 16.0 / float(N**3)
    row = lax.broadcasted_iota(jnp.int32, (N, N), 0)
    column = lax.broadcasted_iota(jnp.int32, (N, N), 1)
    row = jnp.minimum(row, N - row)
    column = jnp.minimum(column, N - column)
    plane = row * row + column * column
    zero_mode = jnp.logical_and(lax.broadcasted_iota(jnp.int32, (1, N), 1) == 0, core == 0)

    def table(i, _):
        ky = core * H + i
        ky = jnp.minimum(ky, N - ky)
        d = (plane + ky * ky).astype(F32)
        vt[pl.ds(pl.multiple_of(i * N, N), N), :] = jnp.where(d > 0, strength / jnp.maximum(d, 1.0), 0.0)
        return 0

    lax.fori_loop(0, H, table, 0)
    own_copy.wait()
    forward(0, OH, OH, 0)
    forward(0, OH, OH, 1)

    arrived(T_OX)
    start(T_MXA, T_QXA, T_MXB, T_QXB)
    arrived(T_PX)
    start(T_PHA)
    arrived(T_MH, T_QH)
    start(T_RX, T_RX + 1, T_PHB)
    start(*range(T_RX + 2, T_RX + CHUNKS))
    start(T_RXZ)
    forward(0, OX, OX, 2)
    forward(0, OX, OX, 3)
    finish(0, OH, 0, first=True)
    pass_on(0)
    pass_on(1)
    forward(0, OX, PX, 2)
    forward(0, OX, PX, 3)
    forward(1, OH, MH, 0)
    forward(1, OH, MH, 1)
    forward(2, OH, QH, 0)
    forward(2, OH, QH, 1)
    arrived(T_PHA)
    forward(0, OH, PH, 0)
    arrived(T_MXA)
    forward(1, OX, MX, 2)
    arrived(T_QXA)
    forward(2, OX, QX, 2)
    arrived(T_PHB)
    start(T_RHZ)
    forward(0, OH, PH, 1)
    finish(0, PH, 1, between=lambda: pass_on(2))
    pass_on(3)
    forward(0, OX, RX, 2)
    arrived(T_MXB)
    forward(1, OX, MX, 3)
    finish(1, MH, 0, between=lambda: pass_on(4))
    arrived(T_QXB)
    forward(2, OX, QX, 3)
    finish(2, QH, 1, between=lambda: pass_on(5))
    for k in range(6, CHUNKS):
        pass_on(k)
    arrived(T_RXZ)
    forward(0, OX, RX, 3)
    arrived(*range(T_RH, T_RH + 4))
    forward(0, OH, RH, 0)
    arrived(*range(T_RH + 4, T_RH + CHUNKS), T_RHZ)
    forward(0, OH, RH, 1)
    finish(0, RH, 0)
    for t in range(T_COUNT):
        moves[t].wait_send()


def halves(matrix):
    high = matrix.astype(ml_dtypes.bfloat16)
    low = (matrix - high.astype(np.float64)).astype(ml_dtypes.bfloat16)
    return high, low


def left_weight(matrix):
    high, low = halves(matrix)
    return np.concatenate(
        [np.concatenate([high, high], axis=1), np.concatenate([low, np.zeros_like(low)], axis=1)], axis=0
    )


def tables():
    index = np.arange(N)
    angle = 2.0 * np.pi / N * (index[:, None] * index[None, :] % N)
    cas = np.cos(angle) + np.sin(angle)
    high, low = halves(cas)
    wz = np.concatenate(
        [np.concatenate([high, low], axis=1), np.concatenate([high, np.zeros_like(low)], axis=1)], axis=0
    )
    order = [np.concatenate([index[c * H : c * H + H], index[H - c * H : N - c * H]]) for c in (0, 1)]
    wy = np.stack([left_weight(cas[order[c]]) for c in (0, 1)])
    wyi = np.stack([left_weight(cas[:, order[c]]) for c in (0, 1)])
    wx = left_weight(cas)
    kept = [np.concatenate([index[:Q], index[Q : 2 * Q]]), np.concatenate([index[:Q], index[3 * Q :]])]
    wxi = np.stack([left_weight(cas[kept[c]]) for c in (0, 1)])
    return wz, wy, wx, wxi, wyi


def on_device(orbitals):
    weights = [jnp.asarray(w) for w in tables()]
    vmem = pl.BlockSpec(memory_space=pltpu.VMEM)
    return pl.pallas_call(
        kernel,
        out_shape=jax.ShapeDtypeStruct(orbitals.shape, F32),
        in_specs=[pl.BlockSpec(memory_space=pl.ANY)] + [vmem] * 5,
        out_specs=vmem,
        scratch_shapes=[
            pltpu.VMEM((10, Q, N, N), F32),
            pltpu.VMEM((SETS, N * H, N), F32),
            pltpu.VMEM((SETS, 4, H * PART, N), F32),
            pltpu.VMEM((2, Q * H // 2, N), F32),
            pltpu.VMEM((2, 2, Q * H // 2, N), F32),
            pltpu.VMEM((2, Q * H // 2, N), F32),
            pltpu.VMEM((H * N, N), F32),
            pltpu.SemaphoreType.DMA((T_COUNT,)),
            pltpu.SemaphoreType.DMA((T_COUNT,)),
            pltpu.SemaphoreType.DMA((SETS * 4,)),
            pltpu.SemaphoreType.DMA((SETS * 4,)),
            pltpu.SemaphoreType.DMA((4,)),
            pltpu.SemaphoreType.DMA((4,)),
            pltpu.SemaphoreType.DMA,
        ],
        compiler_params=pltpu.CompilerParams(
            collective_id=0, has_side_effects=True, vmem_limit_bytes=60 * 1024 * 1024
        ),
    )(orbitals, *weights)


def solution(mesh):
    spec = P("band", "grid", None, None)
    return jax.shard_map(on_device, mesh=mesh, in_specs=(spec,), out_specs=spec, check_vma=False)
```

```python
import functools
import math

import jax
import jax.numpy as jnp
import ml_dtypes
import numpy as np
from jax import lax
from jax.experimental import pallas as pl
from jax.experimental.pallas import tpu as pltpu
from jax.sharding import PartitionSpec as P

MESH = pl.DeviceIdType.MESH
BF16 = jnp.bfloat16
F32 = jnp.float32
N = 128
Q = 32
H = 64

OH, OX, PH, PX, MH, MX, QH, QX, RH, RX = range(10)
PART = 16
CH = 4
CHUNKS = 7
ZROWS = CHUNKS * CH
T_OX, T_PX, T_MH, T_QH, T_MXA, T_MXB, T_QXA, T_QXB, T_PHA, T_PHB, T_RXZ, T_RHZ = range(12)
T_RX = 12
T_RH = T_RX + CHUNKS
T_COUNT = T_RH + CHUNKS
SETS = 3
UNROLL = 8
WIDE = 16


def split(value):
    high = value.astype(BF16)
    low = (value - high.astype(F32)).astype(BF16)
    return high, low


def mm(a, b):
    return jnp.dot(a, b, preferred_element_type=F32)


def stacked(value):
    high, low = split(value)
    return jnp.concatenate([high, low], axis=0)


def kernel(x_ref, wz, wy, wx, wxi, wyi, out_ref, orb, spec, send, ga, gb, back, vt, ssem, rsem, esem, fsem, bsem, csem, lsem):
    band = lax.axis_index("band")
    grid = lax.axis_index("grid")
    bands = lax.axis_size("band")
    core = grid % 2
    side = band % 2
    mate = (band, grid + 1 - 2 * core)
    near = (band, (grid + 2) % 4)
    cross = (band + 1 - 2 * side, (grid + 2) % 4)
    up = ((band + 2) % bands, grid)
    down = ((band + bands - 2) % bands, grid)
    beyond = (jnp.where(side == 0, up[0], down[0]), grid)

    own_copy = pltpu.make_async_copy(x_ref.at[0], orb.at[OH], lsem)
    own_copy.start()
    barrier = pltpu.get_barrier_semaphore()
    for other in (mate, near, cross, up, down):
        pl.semaphore_signal(barrier, inc=1, device_id=other, device_id_type=MESH)
    pl.semaphore_wait(barrier, 5)

    def remote(src, dst, send_sem, recv_sem, device):
        return pltpu.make_async_remote_copy(
            src_ref=src, dst_ref=dst, send_sem=send_sem, recv_sem=recv_sem, device_id=device, device_id_type=MESH
        )

    moves = {}

    def transfer(index, src, dst, device):
        moves[index] = remote(src, dst, ssem.at[index], rsem.at[index], device)

    def passed_on(index, src_slot, dst_slot, first, count, device):
        rows = pl.ds(first, count)
        transfer(index, orb.at[src_slot, rows], orb.at[dst_slot, rows], device)

    transfer(T_OX, x_ref.at[0], orb.at[OX], near)
    transfer(T_PX, x_ref.at[0], orb.at[PX], cross)
    transfer(T_MH, x_ref.at[0], orb.at[MH], up)
    transfer(T_QH, x_ref.at[0], orb.at[QH], down)
    passed_on(T_MXA, OX, MX, 0, PART, up)
    passed_on(T_MXB, OX, MX, PART, PART, up)
    passed_on(T_QXA, OX, QX, 0, PART, down)
    passed_on(T_QXB, OX, QX, PART, PART, down)
    passed_on(T_PHA, PX, PH, 0, PART, near)
    passed_on(T_PHB, OX, PH, PART, PART, cross)
    passed_on(T_RXZ, PX, RX, ZROWS, Q - ZROWS, beyond)
    passed_on(T_RHZ, PH, RH, ZROWS, Q - ZROWS, beyond)
    far_source = jnp.where(side == 0, QH, MH)
    for k in range(CHUNKS):
        passed_on(T_RX + k, far_source, RX, k * CH, CH, cross)
        passed_on(T_RH + k, RX, RH, k * CH, CH, near)

    block = H * PART
    first_mate = jnp.where(core == 0, 6, 2) * block
    second_mate = jnp.where(core == 0, 2, 6) * block

    def swap(s, part):
        at = (first_mate if part < 2 else second_mate) + (part % 2) * block
        sem = s * 4 + part
        return remote(send.at[s, part], spec.at[s, pl.ds(at, block)], esem.at[sem], fsem.at[sem], mate)

    swaps = {(s, part): swap(s, part) for s in range(SETS) for part in range(4)}
    backs = {
        (turn, c): remote(
            back.at[c], gb.at[turn, c], bsem.at[turn * 2 + c], csem.at[turn * 2 + c], mate
        )
        for turn in range(2)
        for c in range(2)
    }

    def forward(s, o_slot, j_slot, part):
        first = (part % 2) * PART
        keep = (part % 2 + part // 2 * 4) * block

        def step(i, _):
            a = i * 2
            rho = (orb[o_slot, pl.ds(first + a, 2)] * orb[j_slot, pl.ds(first + a, 2)]).reshape(2 * N, N)
            high, low = split(rho)
            t = mm(jnp.concatenate([high, low], axis=1), wz[...])
            t = t[:, :N] + t[:, N:]
            u = mm(wy[core], stacked(jnp.concatenate([t[:N], t[N:]], axis=1)))
            u = u[:N] + u[N:]
            for b in range(2):
                plane = u[:, b * N : b * N + N]
                spec[s, pl.ds(keep + a + b, H, stride=PART), :] = plane[:H]
                send[s, part, pl.ds(a + b, H, stride=PART), :] = plane[H:]
            return 0

        lax.fori_loop(0, PART // 2, step, 0, unroll=UNROLL)
        swaps[s, part].start()

    def row_of(s, k):
        return jnp.concatenate(
            [spec[s, pl.ds(pl.multiple_of(p * block + k * PART, PART), PART), :] for p in range(8)], axis=0
        )

    def along_x(s, turn, c):
        if c == 0:
            column = row_of(s, 0)
            column = column - jnp.where(zero_mode, jnp.mean(column, axis=0, keepdims=True), 0.0)
            for p in range(8):
                spec[s, pl.ds(p * block, PART), :] = column[p * PART : p * PART + PART]

        def step(i, _):
            k = c * (H // 2) + i * WIDE
            m = jnp.concatenate([row_of(s, k + b) for b in range(WIDE)], axis=1)
            f = mm(wx[...], stacked(m))
            v = jnp.concatenate([vt[pl.ds(pl.multiple_of((k + b) * N, N), N), :] for b in range(WIDE)], axis=1)
            f = (f[:N] + f[N:]) * v
            r = mm(wxi[core], stacked(f))
            r = r[:H] + r[H:]
            for b in range(WIDE):
                plane = r[:, b * N : b * N + N]
                ga[c, pl.ds(i * WIDE + b, Q, stride=H // 2), :] = plane[:Q]
                back[c, pl.ds(i * WIDE + b, Q, stride=H // 2), :] = plane[Q:]
            return 0

        lax.fori_loop(0, H // 2 // WIDE, step, 0, unroll=2)
        backs[turn, c].start()

    def inverse(j_slot, turn, first):
        def step(i, _):
            a = i * 2
            planes = []
            for b in range(2):
                rows = pl.ds(pl.multiple_of((a + b) * (H // 2), H // 2), H // 2)
                planes.append(
                    jnp.concatenate([ga[0, rows, :], ga[1, rows, :], gb[turn, 0, rows, :], gb[turn, 1, rows, :]], axis=0)
                )
            t = mm(wyi[core], stacked(jnp.concatenate(planes, axis=1)))
            t = t[:N] + t[N:]
            high, low = split(jnp.concatenate([t[:, :N], t[:, N:]], axis=0))
            w = mm(jnp.concatenate([high, low], axis=1), wz[...])
            w = (w[:, :N] + w[:, N:]).reshape(2, N, N) * orb[j_slot, pl.ds(a, 2)]
            if first:
                out_ref[0, pl.ds(a, 2)] = -w
            else:
                out_ref[0, pl.ds(a, 2)] -= w
            return 0

        lax.fori_loop(0, Q // 2, step, 0, unroll=UNROLL)

    def finish(s, j_slot, turn, between=lambda: None, first=False):
        for part in (2, 3, 0, 1):
            swaps[s, part].wait()
        along_x(s, turn, 0)
        along_x(s, turn, 1)
        between()
        backs[turn, 0].wait()
        backs[turn, 1].wait()
        inverse(j_slot, turn, first)

    def arrived(*indices):
        for t in indices:
            moves[t].wait_recv()

    def start(*indices):
        for t in indices:
            moves[t].start()

    def pass_on(k):
        arrived(T_RX + k)
        start(T_RH + k)

    start(T_OX, T_PX, T_MH, T_QH)

    strength = N * math.sqrt(N) / 16.0 / float(N**3)
    row = lax.broadcasted_iota(jnp.int32, (N, N), 0)
    column = lax.broadcasted_iota(jnp.int32, (N, N), 1)
    row = jnp.minimum(row, N - row)
    column = jnp.minimum(column, N - column)
    plane = row * row + column * column
    zero_mode = jnp.logical_and(lax.broadcasted_iota(jnp.int32, (1, N), 1) == 0, core == 0)

    def table(i, _):
        ky = core * H + i
        ky = jnp.minimum(ky, N - ky)
        d = (plane + ky * ky).astype(F32)
        vt[pl.ds(pl.multiple_of(i * N, N), N), :] = jnp.where(d > 0, strength / jnp.maximum(d, 1.0), 0.0)
        return 0

    lax.fori_loop(0, H, table, 0)
    own_copy.wait()
    forward(0, OH, OH, 0)
    forward(0, OH, OH, 1)

    arrived(T_OX)
    start(T_MXA, T_QXA, T_MXB, T_QXB)
    arrived(T_PX)
    start(T_PHA)
    arrived(T_MH, T_QH)
    start(T_RX, T_RX + 1, T_PHB)
    start(*range(T_RX + 2, T_RX + CHUNKS))
    start(T_RXZ)
    forward(0, OX, OX, 2)
    forward(0, OX, OX, 3)
    finish(0, OH, 0, first=True)
    pass_on(0)
    pass_on(1)
    forward(0, OX, PX, 2)
    forward(0, OX, PX, 3)
    forward(1, OH, MH, 0)
    forward(1, OH, MH, 1)
    forward(2, OH, QH, 0)
    forward(2, OH, QH, 1)
    arrived(T_PHA)
    forward(0, OH, PH, 0)
    arrived(T_MXA)
    forward(1, OX, MX, 2)
    arrived(T_QXA)
    forward(2, OX, QX, 2)
    arrived(T_PHB)
    start(T_RHZ)
    forward(0, OH, PH, 1)
    finish(0, PH, 1, between=lambda: pass_on(2))
    pass_on(3)
    forward(0, OX, RX, 2)
    arrived(T_MXB)
    forward(1, OX, MX, 3)
    finish(1, MH, 0, between=lambda: pass_on(4))
    arrived(T_QXB)
    forward(2, OX, QX, 3)
    finish(2, QH, 1, between=lambda: pass_on(5))
    for k in range(6, CHUNKS):
        pass_on(k)
    arrived(T_RXZ)
    forward(0, OX, RX, 3)
    arrived(*range(T_RH, T_RH + 4))
    forward(0, OH, RH, 0)
    arrived(*range(T_RH + 4, T_RH + CHUNKS), T_RHZ)
    forward(0, OH, RH, 1)
    finish(0, RH, 0)
    for t in range(T_COUNT):
        moves[t].wait_send()


def halves(matrix):
    high = matrix.astype(ml_dtypes.bfloat16)
    low = (matrix - high.astype(np.float64)).astype(ml_dtypes.bfloat16)
    return high, low


def left_weight(matrix):
    high, low = halves(matrix)
    return np.concatenate(
        [np.concatenate([high, high], axis=1), np.concatenate([low, np.zeros_like(low)], axis=1)], axis=0
    )


def tables():
    index = np.arange(N)
    angle = 2.0 * np.pi / N * (index[:, None] * index[None, :] % N)
    cas = np.cos(angle) + np.sin(angle)
    high, low = halves(cas)
    wz = np.concatenate(
        [np.concatenate([high, low], axis=1), np.concatenate([high, np.zeros_like(low)], axis=1)], axis=0
    )
    order = [np.concatenate([index[c * H : c * H + H], index[H - c * H : N - c * H]]) for c in (0, 1)]
    wy = np.stack([left_weight(cas[order[c]]) for c in (0, 1)])
    wyi = np.stack([left_weight(cas[:, order[c]]) for c in (0, 1)])
    wx = left_weight(cas)
    kept = [np.concatenate([index[:Q], index[Q : 2 * Q]]), np.concatenate([index[:Q], index[3 * Q :]])]
    wxi = np.stack([left_weight(cas[kept[c]]) for c in (0, 1)])
    return wz, wy, wx, wxi, wyi


def on_device(orbitals):
    weights = [jnp.asarray(w) for w in tables()]
    vmem = pl.BlockSpec(memory_space=pltpu.VMEM)
    return pl.pallas_call(
        kernel,
        out_shape=jax.ShapeDtypeStruct(orbitals.shape, F32),
        in_specs=[pl.BlockSpec(memory_space=pl.ANY)] + [vmem] * 5,
        out_specs=vmem,
        scratch_shapes=[
            pltpu.VMEM((10, Q, N, N), F32),
            pltpu.VMEM((SETS, N * H, N), F32),
            pltpu.VMEM((SETS, 4, H * PART, N), F32),
            pltpu.VMEM((2, Q * H // 2, N), F32),
            pltpu.VMEM((2, 2, Q * H // 2, N), F32),
            pltpu.VMEM((2, Q * H // 2, N), F32),
            pltpu.VMEM((H * N, N), F32),
            pltpu.SemaphoreType.DMA((T_COUNT,)),
            pltpu.SemaphoreType.DMA((T_COUNT,)),
            pltpu.SemaphoreType.DMA((SETS * 4,)),
            pltpu.SemaphoreType.DMA((SETS * 4,)),
            pltpu.SemaphoreType.DMA((4,)),
            pltpu.SemaphoreType.DMA((4,)),
            pltpu.SemaphoreType.DMA,
        ],
        compiler_params=pltpu.CompilerParams(
            collective_id=0, has_side_effects=True, vmem_limit_bytes=60 * 1024 * 1024
        ),
    )(orbitals, *weights)


def solution(mesh):
    spec = P("band", "grid", None, None)
    return jax.shard_map(on_device, mesh=mesh, in_specs=(spec,), out_specs=spec, check_vma=False)
```

```python
import functools
import math

import jax
import jax.numpy as jnp
import ml_dtypes
import numpy as np
from jax import lax
from jax.experimental import pallas as pl
from jax.experimental.pallas import tpu as pltpu
from jax.sharding import PartitionSpec as P

MESH = pl.DeviceIdType.MESH
BF16 = jnp.bfloat16
F32 = jnp.float32
N = 128
Q = 32
H = 64

OH, OX, PH, PX, MH, MX, QH, QX, RH, RX = range(10)
PART = 16
CH = 2
CHUNKS = 13
ZROWS = CHUNKS * CH
EARLY = 4
(
    T_OXA, T_OXB, T_PXA, T_PXB, T_MHA, T_MHB, T_QHA, T_QHB,
    T_MXA, T_MXB, T_QXA, T_QXB, T_PHA, T_PHB, T_RXZ, T_RHZ,
) = range(16)
T_RX = 16
T_RH = T_RX + CHUNKS
T_COUNT = T_RH + CHUNKS
SETS = 3
UNROLL = 8
WIDE = 16


def split(value):
    high = value.astype(BF16)
    low = (value - high.astype(F32)).astype(BF16)
    return high, low


def mm(a, b):
    return jnp.dot(a, b, preferred_element_type=F32)


def stacked(value):
    high, low = split(value)
    return jnp.concatenate([high, low], axis=0)


def kernel(x_ref, wz, wy, wx, wxi, wyi, out_ref, orb, spec, send, ga, gb, back, vt, ssem, rsem, esem, fsem, bsem, csem, lsem):
    band = lax.axis_index("band")
    grid = lax.axis_index("grid")
    bands = lax.axis_size("band")
    core = grid % 2
    side = band % 2
    mate = (band, grid + 1 - 2 * core)
    near = (band, (grid + 2) % 4)
    cross = (band + 1 - 2 * side, (grid + 2) % 4)
    up = ((band + 2) % bands, grid)
    down = ((band + bands - 2) % bands, grid)
    beyond = (jnp.where(side == 0, up[0], down[0]), grid)

    own_copy = pltpu.make_async_copy(x_ref.at[0], orb.at[OH], lsem)
    own_copy.start()
    barrier = pltpu.get_barrier_semaphore()
    for other in (mate, near, cross, up, down):
        pl.semaphore_signal(barrier, inc=1, device_id=other, device_id_type=MESH)
    pl.semaphore_wait(barrier, 5)

    def remote(src, dst, send_sem, recv_sem, device):
        return pltpu.make_async_remote_copy(
            src_ref=src, dst_ref=dst, send_sem=send_sem, recv_sem=recv_sem, device_id=device, device_id_type=MESH
        )

    moves = {}

    def transfer(index, src, dst, device):
        moves[index] = remote(src, dst, ssem.at[index], rsem.at[index], device)

    def passed_on(index, src_slot, dst_slot, first, count, device):
        rows = pl.ds(first, count)
        transfer(index, orb.at[src_slot, rows], orb.at[dst_slot, rows], device)

    for index, slot, device in ((T_OXA, OX, near), (T_PXA, PX, cross), (T_MHA, MH, up), (T_QHA, QH, down)):
        for part in range(2):
            rows = pl.ds(part * PART, PART)
            transfer(index + part, x_ref.at[0, rows], orb.at[slot, rows], device)
    passed_on(T_MXA, OX, MX, 0, PART, up)
    passed_on(T_MXB, OX, MX, PART, PART, up)
    passed_on(T_QXA, OX, QX, 0, PART, down)
    passed_on(T_QXB, OX, QX, PART, PART, down)
    passed_on(T_PHA, PX, PH, 0, PART, near)
    passed_on(T_PHB, OX, PH, PART, PART, cross)
    passed_on(T_RXZ, PX, RX, ZROWS, Q - ZROWS, beyond)
    passed_on(T_RHZ, PH, RH, ZROWS, Q - ZROWS, beyond)
    far_source = jnp.where(side == 0, QH, MH)
    for k in range(CHUNKS):
        passed_on(T_RX + k, far_source, RX, k * CH, CH, cross)
        passed_on(T_RH + k, RX, RH, k * CH, CH, near)

    block = H * PART
    first_mate = jnp.where(core == 0, 6, 2) * block
    second_mate = jnp.where(core == 0, 2, 6) * block

    def swap(s, part):
        at = (first_mate if part < 2 else second_mate) + (part % 2) * block
        sem = s * 4 + part
        return remote(send.at[s, part], spec.at[s, pl.ds(at, block)], esem.at[sem], fsem.at[sem], mate)

    swaps = {(s, part): swap(s, part) for s in range(SETS) for part in range(4)}
    backs = {
        (turn, c): remote(
            back.at[turn, c], gb.at[turn, c], bsem.at[turn * 2 + c], csem.at[turn * 2 + c], mate
        )
        for turn in range(2)
        for c in range(2)
    }

    def forward(s, o_slot, j_slot, part):
        first = (part % 2) * PART
        keep = (part % 2 + part // 2 * 4) * block

        def step(i, _):
            a = i * 2
            rho = (orb[o_slot, pl.ds(first + a, 2)] * orb[j_slot, pl.ds(first + a, 2)]).reshape(2 * N, N)
            high, low = split(rho)
            t = mm(jnp.concatenate([high, low], axis=1), wz[...])
            t = t[:, :N] + t[:, N:]
            u = mm(wy[core], stacked(jnp.concatenate([t[:N], t[N:]], axis=1)))
            u = u[:N] + u[N:]
            for b in range(2):
                plane = u[:, b * N : b * N + N]
                spec[s, pl.ds(keep + a + b, H, stride=PART), :] = plane[:H]
                send[s, part, pl.ds(a + b, H, stride=PART), :] = plane[H:]
            return 0

        lax.fori_loop(0, PART // 2, step, 0, unroll=UNROLL)
        swaps[s, part].start()

    def row_of(s, k):
        return jnp.concatenate(
            [spec[s, pl.ds(pl.multiple_of(p * block + k * PART, PART), PART), :] for p in range(8)], axis=0
        )

    def along_x(s, turn, c):
        if c == 0:
            column = row_of(s, 0)
            column = column - jnp.where(zero_mode, jnp.mean(column, axis=0, keepdims=True), 0.0)
            for p in range(8):
                spec[s, pl.ds(p * block, PART), :] = column[p * PART : p * PART + PART]

        def step(i, _):
            k = c * (H // 2) + i * WIDE
            m = jnp.concatenate([row_of(s, k + b) for b in range(WIDE)], axis=1)
            f = mm(wx[...], stacked(m))
            v = jnp.concatenate([vt[pl.ds(pl.multiple_of((k + b) * N, N), N), :] for b in range(WIDE)], axis=1)
            f = (f[:N] + f[N:]) * v
            r = mm(wxi[core], stacked(f))
            r = r[:H] + r[H:]
            for b in range(WIDE):
                plane = r[:, b * N : b * N + N]
                ga[turn, c, pl.ds(i * WIDE + b, Q, stride=H // 2), :] = plane[:Q]
                back[turn, c, pl.ds(i * WIDE + b, Q, stride=H // 2), :] = plane[Q:]
            return 0

        lax.fori_loop(0, H // 2 // WIDE, step, 0, unroll=2)
        backs[turn, c].start()

    def inverse(j_slot, turn, first=False):
        backs[turn, 0].wait()
        backs[turn, 1].wait()

        def step(i, _):
            a = i * 2
            planes = []
            for b in range(2):
                rows = pl.ds(pl.multiple_of((a + b) * (H // 2), H // 2), H // 2)
                planes.append(
                    jnp.concatenate([ga[turn, 0, rows, :], ga[turn, 1, rows, :], gb[turn, 0, rows, :], gb[turn, 1, rows, :]], axis=0)
                )
            t = mm(wyi[core], stacked(jnp.concatenate(planes, axis=1)))
            t = t[:N] + t[N:]
            high, low = split(jnp.concatenate([t[:, :N], t[:, N:]], axis=0))
            w = mm(jnp.concatenate([high, low], axis=1), wz[...])
            w = (w[:, :N] + w[:, N:]).reshape(2, N, N) * orb[j_slot, pl.ds(a, 2)]
            if first:
                out_ref[0, pl.ds(a, 2)] = -w
            else:
                out_ref[0, pl.ds(a, 2)] -= w
            return 0

        lax.fori_loop(0, Q // 2, step, 0, unroll=UNROLL)

    def spectrum(s, turn):
        for part in (2, 3, 0, 1):
            swaps[s, part].wait()
        along_x(s, turn, 0)
        along_x(s, turn, 1)

    def arrived(*indices):
        for t in indices:
            moves[t].wait_recv()

    def start(*indices):
        for t in indices:
            moves[t].start()

    def pass_on(*chunks):
        for k in chunks:
            arrived(T_RX + k)
            start(T_RH + k)

    start(T_OXA, T_PXA, T_MHA, T_QHA, T_OXB, T_PXB, T_MHB, T_QHB)

    strength = N * math.sqrt(N) / 16.0 / float(N**3)
    row = lax.broadcasted_iota(jnp.int32, (N, N), 0)
    column = lax.broadcasted_iota(jnp.int32, (N, N), 1)
    row = jnp.minimum(row, N - row)
    column = jnp.minimum(column, N - column)
    plane = row * row + column * column
    zero_mode = jnp.logical_and(lax.broadcasted_iota(jnp.int32, (1, N), 1) == 0, core == 0)

    def table(i, _):
        ky = core * H + i
        ky = jnp.minimum(ky, N - ky)
        d = (plane + ky * ky).astype(F32)
        vt[pl.ds(pl.multiple_of(i * N, N), N), :] = jnp.where(d > 0, strength / jnp.maximum(d, 1.0), 0.0)
        return 0

    lax.fori_loop(0, H, table, 0)
    own_copy.wait()
    forward(0, OH, OH, 0)
    forward(0, OH, OH, 1)

    arrived(T_OXA)
    start(T_MXA, T_QXA)
    arrived(T_PXA)
    start(T_PHA)
    arrived(T_MHA, T_QHA)
    start(*range(T_RX, T_RX + EARLY))
    forward(0, OX, OX, 2)
    forward(1, OH, MH, 0)
    forward(2, OH, QH, 0)
    arrived(T_OXB)
    start(T_MXB, T_QXB, T_PHB)
    arrived(T_PXB)
    start(T_RXZ)
    arrived(T_MHB, T_QHB)
    start(*range(T_RX + EARLY, T_RX + CHUNKS))
    forward(0, OX, OX, 3)
    forward(1, OH, MH, 1)
    forward(2, OH, QH, 1)
    spectrum(0, 0)
    pass_on(0, 1)
    inverse(OH, 0, first=True)
    pass_on(2, 3)
    forward(0, OX, PX, 2)
    forward(0, OX, PX, 3)
    arrived(T_PHA)
    forward(0, OH, PH, 0)
    arrived(T_MXA)
    forward(1, OX, MX, 2)
    arrived(T_QXA)
    forward(2, OX, QX, 2)
    arrived(T_PHB)
    start(T_RHZ)
    forward(0, OH, PH, 1)
    pass_on(4)
    spectrum(0, 1)
    pass_on(5)
    inverse(PH, 1)
    pass_on(6, 7)
    forward(0, OX, RX, 2)
    arrived(T_MXB)
    forward(1, OX, MX, 3)
    arrived(T_QXB)
    forward(2, OX, QX, 3)
    spectrum(1, 0)
    pass_on(8)
    spectrum(2, 1)
    pass_on(9)
    inverse(MH, 0)
    pass_on(10)
    inverse(QH, 1)
    pass_on(11)
    arrived(*range(T_RH, T_RH + 8))
    forward(0, OH, RH, 0)
    pass_on(12)
    arrived(T_RXZ)
    forward(0, OX, RX, 3)
    arrived(*range(T_RH + 8, T_RH + CHUNKS), T_RHZ)
    forward(0, OH, RH, 1)
    spectrum(0, 0)
    inverse(RH, 0)
    for t in range(T_COUNT):
        moves[t].wait_send()


def halves(matrix):
    high = matrix.astype(ml_dtypes.bfloat16)
    low = (matrix - high.astype(np.float64)).astype(ml_dtypes.bfloat16)
    return high, low


def left_weight(matrix):
    high, low = halves(matrix)
    return np.concatenate(
        [np.concatenate([high, high], axis=1), np.concatenate([low, np.zeros_like(low)], axis=1)], axis=0
    )


def tables():
    index = np.arange(N)
    angle = 2.0 * np.pi / N * (index[:, None] * index[None, :] % N)
    cas = np.cos(angle) + np.sin(angle)
    high, low = halves(cas)
    wz = np.concatenate(
        [np.concatenate([high, low], axis=1), np.concatenate([high, np.zeros_like(low)], axis=1)], axis=0
    )
    order = [np.concatenate([index[c * H : c * H + H], index[H - c * H : N - c * H]]) for c in (0, 1)]
    wy = np.stack([left_weight(cas[order[c]]) for c in (0, 1)])
    wyi = np.stack([left_weight(cas[:, order[c]]) for c in (0, 1)])
    wx = left_weight(cas)
    kept = [np.concatenate([index[:Q], index[Q : 2 * Q]]), np.concatenate([index[:Q], index[3 * Q :]])]
    wxi = np.stack([left_weight(cas[kept[c]]) for c in (0, 1)])
    return wz, wy, wx, wxi, wyi


def on_device(orbitals):
    weights = [jnp.asarray(w) for w in tables()]
    vmem = pl.BlockSpec(memory_space=pltpu.VMEM)
    return pl.pallas_call(
        kernel,
        out_shape=jax.ShapeDtypeStruct(orbitals.shape, F32),
        in_specs=[pl.BlockSpec(memory_space=pl.ANY)] + [vmem] * 5,
        out_specs=vmem,
        scratch_shapes=[
            pltpu.VMEM((10, Q, N, N), F32),
            pltpu.VMEM((SETS, N * H, N), F32),
            pltpu.VMEM((SETS, 4, H * PART, N), F32),
            pltpu.VMEM((2, 2, Q * H // 2, N), F32),
            pltpu.VMEM((2, 2, Q * H // 2, N), F32),
            pltpu.VMEM((2, 2, Q * H // 2, N), F32),
            pltpu.VMEM((H * N, N), F32),
            pltpu.SemaphoreType.DMA((T_COUNT,)),
            pltpu.SemaphoreType.DMA((T_COUNT,)),
            pltpu.SemaphoreType.DMA((SETS * 4,)),
            pltpu.SemaphoreType.DMA((SETS * 4,)),
            pltpu.SemaphoreType.DMA((4,)),
            pltpu.SemaphoreType.DMA((4,)),
            pltpu.SemaphoreType.DMA,
        ],
        compiler_params=pltpu.CompilerParams(
            collective_id=0, has_side_effects=True, vmem_limit_bytes=60 * 1024 * 1024
        ),
    )(orbitals, *weights)


def solution(mesh):
    spec = P("band", "grid", None, None)
    return jax.shard_map(on_device, mesh=mesh, in_specs=(spec,), out_specs=spec, check_vma=False)
```

```python
import functools
import math

import jax
import jax.numpy as jnp
import ml_dtypes
import numpy as np
from jax import lax
from jax.experimental import pallas as pl
from jax.experimental.pallas import tpu as pltpu
from jax.sharding import PartitionSpec as P

MESH = pl.DeviceIdType.MESH
BF16 = jnp.bfloat16
F32 = jnp.float32
N = 128
Q = 32
H = 64

OH, OX, PH, PX, MH, MX, QH, QX, RH, RX = range(10)
PART = 16
CH = 2
CHUNKS = 13
ZROWS = CHUNKS * CH
EARLY = 4
(
    T_OXA, T_OXB, T_PXA, T_PXB, T_MHA, T_MHB, T_QHA, T_QHB,
    T_MXA, T_MXB, T_QXA, T_QXB, T_PHA, T_PHB, T_RXZ, T_RHZ,
) = range(16)
T_RX = 16
T_RH = T_RX + CHUNKS
T_COUNT = T_RH + CHUNKS
SETS = 3
UNROLL = 8
WIDE = 16


def split(value):
    high = value.astype(BF16)
    low = (value - high.astype(F32)).astype(BF16)
    return high, low


def mm(a, b):
    return jnp.dot(a, b, preferred_element_type=F32)


def stacked(value):
    high, low = split(value)
    return jnp.concatenate([high, low], axis=0)


def kernel(
    x_ref, wz_in, wy_in, wx_in, wxi_in, wyi_in, out_ref,
    orb, spec, send, ga, gb, back, vt, acc, wz, wy, wx, wxi, wyi,
    ssem, rsem, esem, fsem, bsem, csem, lsem,
):
    band = lax.axis_index("band")
    grid = lax.axis_index("grid")
    bands = lax.axis_size("band")
    core = grid % 2
    side = band % 2
    mate = (band, grid + 1 - 2 * core)
    near = (band, (grid + 2) % 4)
    cross = (band + 1 - 2 * side, (grid + 2) % 4)
    up = ((band + 2) % bands, grid)
    down = ((band + bands - 2) % bands, grid)
    beyond = (jnp.where(side == 0, up[0], down[0]), grid)

    fetches = [(x_ref.at[0], orb.at[OH]), (wz_in, wz), (wy_in, wy), (wx_in, wx), (wxi_in, wxi), (wyi_in, wyi)]
    fetches = [pltpu.make_async_copy(src, dst, lsem.at[i]) for i, (src, dst) in enumerate(fetches)]
    barrier = pltpu.get_barrier_semaphore()
    for other in (mate, near, cross, up, down):
        pl.semaphore_signal(barrier, inc=1, device_id=other, device_id_type=MESH)
    pl.semaphore_wait(barrier, 5)

    def remote(src, dst, send_sem, recv_sem, device):
        return pltpu.make_async_remote_copy(
            src_ref=src, dst_ref=dst, send_sem=send_sem, recv_sem=recv_sem, device_id=device, device_id_type=MESH
        )

    moves = {}

    def transfer(index, src, dst, device):
        moves[index] = remote(src, dst, ssem.at[index], rsem.at[index], device)

    def passed_on(index, src_slot, dst_slot, first, count, device):
        rows = pl.ds(first, count)
        transfer(index, orb.at[src_slot, rows], orb.at[dst_slot, rows], device)

    for index, slot, device in ((T_OXA, OX, near), (T_PXA, PX, cross), (T_MHA, MH, up), (T_QHA, QH, down)):
        for part in range(2):
            rows = pl.ds(part * PART, PART)
            transfer(index + part, x_ref.at[0, rows], orb.at[slot, rows], device)
    passed_on(T_MXA, OX, MX, 0, PART, up)
    passed_on(T_MXB, OX, MX, PART, PART, up)
    passed_on(T_QXA, OX, QX, 0, PART, down)
    passed_on(T_QXB, OX, QX, PART, PART, down)
    passed_on(T_PHA, PX, PH, 0, PART, near)
    passed_on(T_PHB, OX, PH, PART, PART, cross)
    passed_on(T_RXZ, PX, RX, ZROWS, Q - ZROWS, beyond)
    passed_on(T_RHZ, PH, RH, ZROWS, Q - ZROWS, beyond)
    far_source = jnp.where(side == 0, QH, MH)
    for k in range(CHUNKS):
        passed_on(T_RX + k, far_source, RX, k * CH, CH, cross)
        passed_on(T_RH + k, RX, RH, k * CH, CH, near)

    block = H * PART
    first_mate = jnp.where(core == 0, 6, 2) * block
    second_mate = jnp.where(core == 0, 2, 6) * block

    def swap(s, part):
        at = (first_mate if part < 2 else second_mate) + (part % 2) * block
        sem = s * 4 + part
        return remote(send.at[s, part], spec.at[s, pl.ds(at, block)], esem.at[sem], fsem.at[sem], mate)

    swaps = {(s, part): swap(s, part) for s in range(SETS) for part in range(4)}

    def give_back(turn, c):
        sem = turn * 2 + c
        return remote(back.at[turn, c], gb.at[turn, c], bsem.at[sem], csem.at[sem], mate)

    def forward(s, o_slot, j_slot, part, begin=0, end=PART // 2):
        first = (part % 2) * PART
        keep = (part % 2 + part // 2 * 4) * block

        def step(i, _):
            a = i * 2
            rho = (orb[o_slot, pl.ds(first + a, 2)] * orb[j_slot, pl.ds(first + a, 2)]).reshape(2 * N, N)
            high, low = split(rho)
            t = mm(jnp.concatenate([high, low], axis=1), wz[...])
            t = t[:, :N] + t[:, N:]
            u = mm(wy[core], stacked(jnp.concatenate([t[:N], t[N:]], axis=1)))
            u = u[:N] + u[N:]
            for b in range(2):
                plane = u[:, b * N : b * N + N]
                spec[s, pl.ds(keep + a + b, H, stride=PART), :] = plane[:H]
                send[s, part, pl.ds(a + b, H, stride=PART), :] = plane[H:]
            return 0

        lax.fori_loop(begin, end, step, 0, unroll=end - begin)
        if end == PART // 2:
            swaps[s, part].start()

    def row_of(s, k):
        return jnp.concatenate(
            [spec[s, pl.ds(pl.multiple_of(p * block + k * PART, PART), PART), :] for p in range(8)], axis=0
        )

    def along_x(s, turn):
        column = row_of(s, 0)
        column = column - jnp.where(zero_mode, jnp.mean(column, axis=0, keepdims=True), 0.0)
        for p in range(8):
            spec[s, pl.ds(p * block, PART), :] = column[p * PART : p * PART + PART]

        def half(c, _):
            def step(i, _):
                k = c * (H // 2) + i * WIDE
                m = jnp.concatenate([row_of(s, k + b) for b in range(WIDE)], axis=1)
                f = mm(wx[...], stacked(m))
                v = jnp.concatenate([vt[pl.ds(pl.multiple_of((k + b) * N, N), N), :] for b in range(WIDE)], axis=1)
                f = (f[:N] + f[N:]) * v
                r = mm(wxi[core], stacked(f))
                r = r[:H] + r[H:]
                for b in range(WIDE):
                    plane = r[:, b * N : b * N + N]
                    ga[turn, c, pl.ds(i * WIDE + b, Q, stride=H // 2), :] = plane[:Q]
                    back[turn, c, pl.ds(i * WIDE + b, Q, stride=H // 2), :] = plane[Q:]
                return 0

            lax.fori_loop(0, H // 2 // WIDE, step, 0, unroll=2)
            give_back(turn, c).start()
            return 0

        lax.fori_loop(0, 2, half, 0)

    def inverse(j_slot, turn, first=False, last=False):
        give_back(turn, 0).wait()
        give_back(turn, 1).wait()

        def step(i, _):
            a = i * 2
            planes = []
            for b in range(2):
                rows = pl.ds(pl.multiple_of((a + b) * (H // 2), H // 2), H // 2)
                planes.append(
                    jnp.concatenate([ga[turn, 0, rows, :], ga[turn, 1, rows, :], gb[turn, 0, rows, :], gb[turn, 1, rows, :]], axis=0)
                )
            t = mm(wyi[core], stacked(jnp.concatenate(planes, axis=1)))
            t = t[:N] + t[N:]
            high, low = split(jnp.concatenate([t[:, :N], t[:, N:]], axis=0))
            w = mm(jnp.concatenate([high, low], axis=1), wz[...])
            w = (w[:, :N] + w[:, N:]).reshape(2, N, N) * orb[j_slot, pl.ds(a, 2)]
            if first:
                acc[pl.ds(a, 2)] = w
            else:
                acc[pl.ds(a, 2)] += w
            return 0

        if not last:
            lax.fori_loop(0, Q // 2, step, 0, unroll=UNROLL)
            return
        stores = []
        for part in range(2):
            lax.fori_loop(part * PART // 2, (part + 1) * PART // 2, step, 0, unroll=PART // 2)
            rows = pl.ds(part * PART, PART)
            stores.append(pltpu.make_async_copy(acc.at[rows], out_ref.at[0, rows], lsem.at[part]))
            stores[part].start()
        for store in stores:
            store.wait()

    def spectrum(s, turn):
        for part in (2, 3, 0, 1):
            swaps[s, part].wait()
        along_x(s, turn)

    def arrived(*indices):
        for t in indices:
            moves[t].wait_recv()

    def start(*indices):
        for t in indices:
            moves[t].start()

    def pass_on(*chunks):
        for k in chunks:
            arrived(T_RX + k)
            start(T_RH + k)

    start(T_OXA, T_PXA, T_MHA, T_QHA, T_OXB, T_PXB, T_MHB, T_QHB)
    for fetch in fetches:
        fetch.start()

    strength = N * math.sqrt(N) / 16.0 / float(N**3)
    row = lax.broadcasted_iota(jnp.int32, (N, N), 0)
    column = lax.broadcasted_iota(jnp.int32, (N, N), 1)
    row = jnp.minimum(row, N - row)
    column = jnp.minimum(column, N - column)
    plane = row * row + column * column
    zero_mode = jnp.logical_and(lax.broadcasted_iota(jnp.int32, (1, N), 1) == 0, core == 0)

    def table(i, _):
        ky = core * H + i
        ky = jnp.minimum(ky, N - ky)
        d = (plane + ky * ky).astype(F32)
        vt[pl.ds(pl.multiple_of(i * N, N), N), :] = jnp.where(d > 0, strength / jnp.maximum(d, 1.0), 0.0)
        return 0

    lax.fori_loop(0, H, table, 0)
    for fetch in fetches:
        fetch.wait()
    forward(0, OH, OH, 0)
    forward(0, OH, OH, 1)

    arrived(T_OXA)
    start(T_MXA, T_QXA)
    arrived(T_PXA)
    start(T_PHA)
    arrived(T_MHA, T_QHA)
    start(*range(T_RX, T_RX + EARLY))
    forward(0, OX, OX, 2)
    forward(1, OH, MH, 0)
    forward(2, OH, QH, 0)
    arrived(T_OXB)
    start(T_MXB, T_QXB, T_PHB)
    arrived(T_PXB)
    start(T_RXZ)
    arrived(T_MHB, T_QHB)
    start(*range(T_RX + EARLY, T_RX + CHUNKS))
    forward(0, OX, OX, 3)
    forward(1, OH, MH, 1)
    forward(2, OH, QH, 1)
    spectrum(0, 0)
    pass_on(0, 1)
    inverse(OH, 0, first=True)
    pass_on(2, 3)
    forward(0, OX, PX, 2)
    forward(0, OX, PX, 3)
    arrived(T_PHA)
    forward(0, OH, PH, 0)
    arrived(T_MXA)
    forward(1, OX, MX, 2)
    arrived(T_QXA)
    forward(2, OX, QX, 2)
    arrived(T_PHB)
    start(T_RHZ)
    forward(0, OH, PH, 1)
    pass_on(4)
    spectrum(0, 1)
    pass_on(5)
    inverse(PH, 1)
    pass_on(6, 7)
    forward(0, OX, RX, 2)
    arrived(T_MXB)
    forward(1, OX, MX, 3)
    arrived(T_QXB)
    forward(2, OX, QX, 3)
    spectrum(1, 0)
    pass_on(8)
    spectrum(2, 1)
    pass_on(9)
    inverse(MH, 0)
    pass_on(10)
    inverse(QH, 1)
    pass_on(11)
    arrived(*range(T_RH, T_RH + 8))
    forward(0, OH, RH, 0)
    pass_on(12)
    over_z = (ZROWS - PART) // 2
    forward(0, OX, RX, 3, end=over_z)
    arrived(T_RXZ)
    forward(0, OX, RX, 3, begin=over_z)
    arrived(*range(T_RH + 8, T_RH + CHUNKS))
    forward(0, OH, RH, 1, end=over_z)
    arrived(T_RHZ)
    forward(0, OH, RH, 1, begin=over_z)
    spectrum(0, 0)
    inverse(RH, 0, last=True)
    for t in range(T_COUNT):
        moves[t].wait_send()


def halves(matrix):
    high = matrix.astype(ml_dtypes.bfloat16)
    low = (matrix - high.astype(np.float64)).astype(ml_dtypes.bfloat16)
    return high, low


def left_weight(matrix):
    high, low = halves(matrix)
    return np.concatenate(
        [np.concatenate([high, high], axis=1), np.concatenate([low, np.zeros_like(low)], axis=1)], axis=0
    )


def tables():
    index = np.arange(N)
    angle = 2.0 * np.pi / N * (index[:, None] * index[None, :] % N)
    cas = np.cos(angle) + np.sin(angle)
    high, low = halves(cas)
    wz = np.concatenate(
        [np.concatenate([high, low], axis=1), np.concatenate([high, np.zeros_like(low)], axis=1)], axis=0
    )
    order = [np.concatenate([index[c * H : c * H + H], index[H - c * H : N - c * H]]) for c in (0, 1)]
    wy = np.stack([left_weight(cas[order[c]]) for c in (0, 1)])
    wyi = np.stack([left_weight(cas[:, order[c]]) for c in (0, 1)])
    wx = left_weight(cas)
    kept = [np.concatenate([index[:Q], index[Q : 2 * Q]]), np.concatenate([index[:Q], index[3 * Q :]])]
    wxi = np.stack([left_weight(cas[kept[c]]) for c in (0, 1)])
    return wz, wy, wx, wxi, wyi


def on_device(orbitals):
    weights = [jnp.asarray(w) for w in tables()]
    total = pl.pallas_call(
        kernel,
        out_shape=jax.ShapeDtypeStruct(orbitals.shape, F32),
        in_specs=[pl.BlockSpec(memory_space=pl.ANY)] * 6,
        out_specs=pl.BlockSpec(memory_space=pl.ANY),
        scratch_shapes=[
            pltpu.VMEM((10, Q, N, N), F32),
            pltpu.VMEM((SETS, N * H, N), F32),
            pltpu.VMEM((SETS, 4, H * PART, N), F32),
            pltpu.VMEM((2, 2, Q * H // 2, N), F32),
            pltpu.VMEM((2, 2, Q * H // 2, N), F32),
            pltpu.VMEM((2, 2, Q * H // 2, N), F32),
            pltpu.VMEM((H * N, N), F32),
            pltpu.VMEM((Q, N, N), F32),
        ]
        + [pltpu.VMEM(w.shape, BF16) for w in weights]
        + [pltpu.SemaphoreType.DMA((n,)) for n in (T_COUNT, T_COUNT, SETS * 4, SETS * 4, 4, 4, 6)],
        compiler_params=pltpu.CompilerParams(
            collective_id=0, has_side_effects=True, vmem_limit_bytes=60 * 1024 * 1024
        ),
    )(orbitals, *weights)
    return -total


def solution(mesh):
    spec = P("band", "grid", None, None)
    return jax.shard_map(on_device, mesh=mesh, in_specs=(spec,), out_specs=spec, check_vma=False)
```

```python
import functools
import math

import jax
import jax.numpy as jnp
import ml_dtypes
import numpy as np
from jax import lax
from jax.experimental import pallas as pl
from jax.experimental.pallas import tpu as pltpu
from jax.sharding import PartitionSpec as P

MESH = pl.DeviceIdType.MESH
BF16 = jnp.bfloat16
F32 = jnp.float32
N = 128
Q = 32
H = 64

OH, OX, PH, PX, MH, MX, QH, QX, RH, RX = range(10)
PART = 16
CH = 2
CHUNKS = 13
ZROWS = CHUNKS * CH
EARLY = 4
(
    T_OXA, T_OXB, T_PXA, T_PXB, T_MHA, T_MHB, T_QHA, T_QHB,
    T_MXA, T_MXB, T_QXA, T_QXB, T_PHA, T_PHB, T_PHC, T_RXZ, T_RHZ,
) = range(17)
T_RX = 17
T_RH = T_RX + CHUNKS
T_COUNT = T_RH + CHUNKS
NEAR_ROWS = 18
SETS = 3
UNROLL = 8
WIDE = 16


def split(value):
    high = value.astype(BF16)
    low = (value - high.astype(F32)).astype(BF16)
    return high, low


def mm(a, b):
    return jnp.dot(a, b, preferred_element_type=F32)


def stacked(value):
    high, low = split(value)
    return jnp.concatenate([high, low], axis=0)


def kernel(
    x_ref, wz_in, wy_in, wx_in, wxi_in, wyi_in, out_ref,
    orb, spec, send, ga, gb, back, vt, acc, wz, wy, wx, wxi, wyi,
    ssem, rsem, esem, fsem, bsem, csem, lsem,
):
    band = lax.axis_index("band")
    grid = lax.axis_index("grid")
    bands = lax.axis_size("band")
    core = grid % 2
    side = band % 2
    mate = (band, grid + 1 - 2 * core)
    near = (band, (grid + 2) % 4)
    cross = (band + 1 - 2 * side, (grid + 2) % 4)
    up = ((band + 2) % bands, grid)
    down = ((band + bands - 2) % bands, grid)
    beyond = (jnp.where(side == 0, up[0], down[0]), grid)

    fetches = [(x_ref.at[0], orb.at[OH]), (wz_in, wz), (wy_in, wy), (wx_in, wx), (wxi_in, wxi), (wyi_in, wyi)]
    fetches = [pltpu.make_async_copy(src, dst, lsem.at[i]) for i, (src, dst) in enumerate(fetches)]
    barrier = pltpu.get_barrier_semaphore()
    for other in (mate, near, cross, up, down):
        pl.semaphore_signal(barrier, inc=1, device_id=other, device_id_type=MESH)
    pl.semaphore_wait(barrier, 5)

    def remote(src, dst, send_sem, recv_sem, device):
        return pltpu.make_async_remote_copy(
            src_ref=src, dst_ref=dst, send_sem=send_sem, recv_sem=recv_sem, device_id=device, device_id_type=MESH
        )

    moves = {}

    def transfer(index, src, dst, device):
        moves[index] = remote(src, dst, ssem.at[index], rsem.at[index], device)

    def passed_on(index, src_slot, dst_slot, first, count, device):
        rows = pl.ds(first, count)
        transfer(index, orb.at[src_slot, rows], orb.at[dst_slot, rows], device)

    for index, slot, device in ((T_OXA, OX, near), (T_PXA, PX, cross), (T_MHA, MH, up), (T_QHA, QH, down)):
        for part in range(2):
            rows = pl.ds(part * PART, PART)
            transfer(index + part, x_ref.at[0, rows], orb.at[slot, rows], device)
    passed_on(T_MXA, OX, MX, 0, PART, up)
    passed_on(T_MXB, OX, MX, PART, PART, up)
    passed_on(T_QXA, OX, QX, 0, PART, down)
    passed_on(T_QXB, OX, QX, PART, PART, down)
    passed_on(T_PHA, PX, PH, 0, PART, near)
    passed_on(T_PHC, PX, PH, PART, NEAR_ROWS - PART, near)
    passed_on(T_PHB, OX, PH, NEAR_ROWS, Q - NEAR_ROWS, cross)
    passed_on(T_RXZ, PX, RX, ZROWS, Q - ZROWS, beyond)
    passed_on(T_RHZ, PH, RH, ZROWS, Q - ZROWS, beyond)
    far_source = jnp.where(side == 0, QH, MH)
    for k in range(CHUNKS):
        passed_on(T_RX + k, far_source, RX, k * CH, CH, cross)
        passed_on(T_RH + k, RX, RH, k * CH, CH, near)

    block = H * PART
    first_mate = jnp.where(core == 0, 6, 2) * block
    second_mate = jnp.where(core == 0, 2, 6) * block

    def swap(s, part):
        at = (first_mate if part < 2 else second_mate) + (part % 2) * block
        sem = s * 4 + part
        return remote(send.at[s, part], spec.at[s, pl.ds(at, block)], esem.at[sem], fsem.at[sem], mate)

    swaps = {(s, part): swap(s, part) for s in range(SETS) for part in range(4)}

    def give_back(turn, c):
        sem = turn * 2 + c
        return remote(back.at[turn, c], gb.at[turn, c], bsem.at[sem], csem.at[sem], mate)

    def forward(s, o_slot, j_slot, part, begin=0, end=PART // 2):
        first = (part % 2) * PART
        keep = (part % 2 + part // 2 * 4) * block

        def step(i, _):
            a = i * 2
            rho = (orb[o_slot, pl.ds(first + a, 2)] * orb[j_slot, pl.ds(first + a, 2)]).reshape(2 * N, N)
            high, low = split(rho)
            t = mm(jnp.concatenate([high, low], axis=1), wz[...])
            t = t[:, :N] + t[:, N:]
            u = mm(wy[core], stacked(jnp.concatenate([t[:N], t[N:]], axis=1)))
            u = u[:N] + u[N:]
            for b in range(2):
                plane = u[:, b * N : b * N + N]
                spec[s, pl.ds(keep + a + b, H, stride=PART), :] = plane[:H]
                send[s, part, pl.ds(a + b, H, stride=PART), :] = plane[H:]
            return 0

        lax.fori_loop(begin, end, step, 0, unroll=end - begin)
        if end == PART // 2:
            swaps[s, part].start()

    def row_of(s, k):
        return jnp.concatenate(
            [spec[s, pl.ds(pl.multiple_of(p * block + k * PART, PART), PART), :] for p in range(8)], axis=0
        )

    def along_x(s, turn):
        column = row_of(s, 0)
        column = column - jnp.where(zero_mode, jnp.mean(column, axis=0, keepdims=True), 0.0)
        for p in range(8):
            spec[s, pl.ds(p * block, PART), :] = column[p * PART : p * PART + PART]

        def half(c, _):
            def step(i, _):
                k = c * (H // 2) + i * WIDE
                m = jnp.concatenate([row_of(s, k + b) for b in range(WIDE)], axis=1)
                f = mm(wx[...], stacked(m))
                v = jnp.concatenate([vt[pl.ds(pl.multiple_of((k + b) * N, N), N), :] for b in range(WIDE)], axis=1)
                f = (f[:N] + f[N:]) * v
                r = mm(wxi[core], stacked(f))
                r = r[:H] + r[H:]
                for b in range(WIDE):
                    plane = r[:, b * N : b * N + N]
                    ga[turn, c, pl.ds(i * WIDE + b, Q, stride=H // 2), :] = plane[:Q]
                    back[turn, c, pl.ds(i * WIDE + b, Q, stride=H // 2), :] = plane[Q:]
                return 0

            lax.fori_loop(0, H // 2 // WIDE, step, 0, unroll=2)
            give_back(turn, c).start()
            return 0

        lax.fori_loop(0, 2, half, 0)

    def inverse(j_slot, turn, first=False, last=False):
        give_back(turn, 0).wait()
        give_back(turn, 1).wait()

        def step(i, _):
            a = i * 2
            planes = []
            for b in range(2):
                rows = pl.ds(pl.multiple_of((a + b) * (H // 2), H // 2), H // 2)
                planes.append(
                    jnp.concatenate([ga[turn, 0, rows, :], ga[turn, 1, rows, :], gb[turn, 0, rows, :], gb[turn, 1, rows, :]], axis=0)
                )
            t = mm(wyi[core], stacked(jnp.concatenate(planes, axis=1)))
            t = t[:N] + t[N:]
            high, low = split(jnp.concatenate([t[:, :N], t[:, N:]], axis=0))
            w = mm(jnp.concatenate([high, low], axis=1), wz[...])
            w = (w[:, :N] + w[:, N:]).reshape(2, N, N) * orb[j_slot, pl.ds(a, 2)]
            if first:
                acc[pl.ds(a, 2)] = w
            else:
                acc[pl.ds(a, 2)] += w
            return 0

        if not last:
            lax.fori_loop(0, Q // 2, step, 0, unroll=UNROLL)
            return
        stores = []
        for part in range(2):
            lax.fori_loop(part * PART // 2, (part + 1) * PART // 2, step, 0, unroll=PART // 2)
            rows = pl.ds(part * PART, PART)
            stores.append(pltpu.make_async_copy(acc.at[rows], out_ref.at[0, rows], lsem.at[part]))
            stores[part].start()
        for store in stores:
            store.wait()

    def spectrum(s, turn):
        for part in (2, 3, 0, 1):
            swaps[s, part].wait()
        along_x(s, turn)

    def arrived(*indices):
        for t in indices:
            moves[t].wait_recv()

    def start(*indices):
        for t in indices:
            moves[t].start()

    def pass_on(*chunks):
        for k in chunks:
            arrived(T_RX + k)
            start(T_RH + k)

    start(T_OXA, T_PXA, T_MHA, T_QHA, T_OXB, T_PXB, T_MHB, T_QHB)
    for fetch in fetches:
        fetch.start()

    strength = N * math.sqrt(N) / 16.0 / float(N**3)
    row = lax.broadcasted_iota(jnp.int32, (N, N), 0)
    column = lax.broadcasted_iota(jnp.int32, (N, N), 1)
    row = jnp.minimum(row, N - row)
    column = jnp.minimum(column, N - column)
    plane = row * row + column * column
    zero_mode = jnp.logical_and(lax.broadcasted_iota(jnp.int32, (1, N), 1) == 0, core == 0)

    def table(i, _):
        ky = core * H + i
        ky = jnp.minimum(ky, N - ky)
        d = (plane + ky * ky).astype(F32)
        vt[pl.ds(pl.multiple_of(i * N, N), N), :] = jnp.where(d > 0, strength / jnp.maximum(d, 1.0), 0.0)
        return 0

    lax.fori_loop(0, H, table, 0)
    for fetch in fetches:
        fetch.wait()
    forward(0, OH, OH, 0)
    forward(0, OH, OH, 1)

    arrived(T_OXA)
    start(T_MXA, T_QXA)
    arrived(T_PXA)
    start(T_PHA)
    arrived(T_MHA, T_QHA)
    start(*range(T_RX, T_RX + EARLY))
    forward(0, OX, OX, 2)
    forward(1, OH, MH, 0)
    forward(2, OH, QH, 0)
    arrived(T_PXB)
    start(T_PHC)
    arrived(T_OXB)
    start(T_MXB, T_QXB, T_PHB)
    arrived(T_MHB, T_QHB)
    start(*range(T_RX + EARLY, T_RX + CHUNKS))
    start(T_RXZ)
    forward(0, OX, OX, 3)
    forward(1, OH, MH, 1)
    forward(2, OH, QH, 1)
    spectrum(0, 0)
    pass_on(0, 1)
    inverse(OH, 0, first=True)
    pass_on(2, 3)
    forward(0, OX, PX, 2)
    forward(0, OX, PX, 3)
    arrived(T_MXA)
    forward(1, OX, MX, 2)
    arrived(T_QXA)
    forward(2, OX, QX, 2)
    arrived(T_PHA)
    forward(0, OH, PH, 0)
    arrived(T_PHC, T_PHB)
    start(T_RHZ)
    forward(0, OH, PH, 1)
    spectrum(0, 1)
    pass_on(4)
    inverse(PH, 1)
    pass_on(5, 6, 7)
    forward(0, OX, RX, 2)
    arrived(T_MXB)
    forward(1, OX, MX, 3)
    pass_on(8)
    arrived(T_QXB)
    forward(2, OX, QX, 3)
    spectrum(1, 0)
    pass_on(9)
    spectrum(2, 1)
    pass_on(10)
    inverse(MH, 0)
    pass_on(11)
    inverse(QH, 1)
    pass_on(12)
    arrived(*range(T_RH, T_RH + 8))
    forward(0, OH, RH, 0)
    over_z = (ZROWS - PART) // 2
    forward(0, OX, RX, 3, end=over_z)
    arrived(T_RXZ)
    forward(0, OX, RX, 3, begin=over_z)
    arrived(*range(T_RH + 8, T_RH + CHUNKS))
    forward(0, OH, RH, 1, end=over_z)
    arrived(T_RHZ)
    forward(0, OH, RH, 1, begin=over_z)
    spectrum(0, 0)
    inverse(RH, 0, last=True)
    for t in range(T_COUNT):
        moves[t].wait_send()


def halves(matrix):
    high = matrix.astype(ml_dtypes.bfloat16)
    low = (matrix - high.astype(np.float64)).astype(ml_dtypes.bfloat16)
    return high, low


def left_weight(matrix):
    high, low = halves(matrix)
    return np.concatenate(
        [np.concatenate([high, high], axis=1), np.concatenate([low, np.zeros_like(low)], axis=1)], axis=0
    )


def tables():
    index = np.arange(N)
    angle = 2.0 * np.pi / N * (index[:, None] * index[None, :] % N)
    cas = np.cos(angle) + np.sin(angle)
    high, low = halves(cas)
    wz = np.concatenate(
        [np.concatenate([high, low], axis=1), np.concatenate([high, np.zeros_like(low)], axis=1)], axis=0
    )
    order = [np.concatenate([index[c * H : c * H + H], index[H - c * H : N - c * H]]) for c in (0, 1)]
    wy = np.stack([left_weight(cas[order[c]]) for c in (0, 1)])
    wyi = np.stack([left_weight(cas[:, order[c]]) for c in (0, 1)])
    wx = left_weight(cas)
    kept = [np.concatenate([index[:Q], index[Q : 2 * Q]]), np.concatenate([index[:Q], index[3 * Q :]])]
    wxi = np.stack([left_weight(cas[kept[c]]) for c in (0, 1)])
    return wz, wy, wx, wxi, wyi


def on_device(orbitals):
    weights = [jnp.asarray(w) for w in tables()]
    total = pl.pallas_call(
        kernel,
        out_shape=pltpu.VMEM(orbitals.shape, F32),
        in_specs=[pl.BlockSpec(memory_space=pl.ANY)] * 6,
        out_specs=pl.BlockSpec(memory_space=pl.ANY),
        scratch_shapes=[
            pltpu.VMEM((10, Q, N, N), F32),
            pltpu.VMEM((SETS, N * H, N), F32),
            pltpu.VMEM((SETS, 4, H * PART, N), F32),
            pltpu.VMEM((2, 2, Q * H // 2, N), F32),
            pltpu.VMEM((2, 2, Q * H // 2, N), F32),
            pltpu.VMEM((2, 2, Q * H // 2, N), F32),
            pltpu.VMEM((H * N, N), F32),
            pltpu.VMEM((Q, N, N), F32),
        ]
        + [pltpu.VMEM(w.shape, BF16) for w in weights]
        + [pltpu.SemaphoreType.DMA((n,)) for n in (T_COUNT, T_COUNT, SETS * 4, SETS * 4, 4, 4, 6)],
        compiler_params=pltpu.CompilerParams(
            collective_id=0, has_side_effects=True, vmem_limit_bytes=60 * 1024 * 1024
        ),
    )(orbitals, *weights)
    return -total


def solution(mesh):
    spec = P("band", "grid", None, None)
    return jax.shard_map(on_device, mesh=mesh, in_specs=(spec,), out_specs=spec, check_vma=False)
```

```python
import functools
import math

import jax
import jax.numpy as jnp
import ml_dtypes
import numpy as np
from jax import lax
from jax.experimental import pallas as pl
from jax.experimental.pallas import tpu as pltpu
from jax.sharding import PartitionSpec as P

MESH = pl.DeviceIdType.MESH
BF16 = jnp.bfloat16
F32 = jnp.float32
N = 128
Q = 32
H = 64

OH, OX, PH, PX, MH, MX, QH, QX, RH, RX = range(10)
PART = 16
CH = 2
CHUNKS = 13
ZROWS = CHUNKS * CH
EARLY = 4
(
    T_OXA, T_OXB, T_PXA, T_PXB, T_MHA, T_MHB, T_QHA, T_QHB,
    T_MXA, T_MXB, T_QXA, T_QXB, T_PHA, T_PHB, T_PHC, T_RXZ, T_RHZ,
) = range(17)
T_RX = 17
T_RH = T_RX + CHUNKS
T_COUNT = T_RH + CHUNKS
NEAR_ROWS = 18
SETS = 3
UNROLL = 8
WIDE = 16


def split(value):
    high = value.astype(BF16)
    low = (value - high.astype(F32)).astype(BF16)
    return high, low


def mm(a, b):
    return jnp.dot(a, b, preferred_element_type=F32)


def stacked(value):
    high, low = split(value)
    return jnp.concatenate([high, low], axis=0)


def kernel(
    x_ref, wz_in, wy_in, wx_in, wxi_in, wyi_in, out_ref,
    orb, spec, send, ga, gb, back, vt, acc, wz, wy, wx, wxi, wyi,
    ssem, rsem, esem, fsem, bsem, csem, lsem,
):
    band = lax.axis_index("band")
    grid = lax.axis_index("grid")
    bands = lax.axis_size("band")
    core = grid % 2
    side = band % 2
    mate = (band, grid + 1 - 2 * core)
    near = (band, (grid + 2) % 4)
    cross = (band + 1 - 2 * side, (grid + 2) % 4)
    up = ((band + 2) % bands, grid)
    down = ((band + bands - 2) % bands, grid)
    beyond = (jnp.where(side == 0, up[0], down[0]), grid)

    fetches = [(x_ref.at[0], orb.at[OH]), (wz_in, wz), (wy_in, wy), (wx_in, wx), (wxi_in, wxi), (wyi_in, wyi)]
    fetches = [pltpu.make_async_copy(src, dst, lsem.at[i]) for i, (src, dst) in enumerate(fetches)]
    barrier = pltpu.get_barrier_semaphore()
    for other in (mate, near, cross, up, down):
        pl.semaphore_signal(barrier, inc=1, device_id=other, device_id_type=MESH)
    pl.semaphore_wait(barrier, 5)

    def remote(src, dst, send_sem, recv_sem, device):
        return pltpu.make_async_remote_copy(
            src_ref=src, dst_ref=dst, send_sem=send_sem, recv_sem=recv_sem, device_id=device, device_id_type=MESH
        )

    moves = {}

    def transfer(index, src, dst, device):
        moves[index] = remote(src, dst, ssem.at[index], rsem.at[index], device)

    def passed_on(index, src_slot, dst_slot, first, count, device):
        rows = pl.ds(first, count)
        transfer(index, orb.at[src_slot, rows], orb.at[dst_slot, rows], device)

    for index, slot, device in ((T_OXA, OX, near), (T_PXA, PX, cross), (T_MHA, MH, up), (T_QHA, QH, down)):
        for part in range(2):
            rows = pl.ds(part * PART, PART)
            transfer(index + part, x_ref.at[0, rows], orb.at[slot, rows], device)
    passed_on(T_MXA, OX, MX, 0, PART, up)
    passed_on(T_MXB, OX, MX, PART, PART, up)
    passed_on(T_QXA, OX, QX, 0, PART, down)
    passed_on(T_QXB, OX, QX, PART, PART, down)
    passed_on(T_PHA, PX, PH, 0, PART, near)
    passed_on(T_PHC, PX, PH, PART, NEAR_ROWS - PART, near)
    passed_on(T_PHB, OX, PH, NEAR_ROWS, Q - NEAR_ROWS, cross)
    passed_on(T_RXZ, PX, RX, ZROWS, Q - ZROWS, beyond)
    passed_on(T_RHZ, PH, RH, ZROWS, Q - ZROWS, beyond)
    far_source = jnp.where(side == 0, QH, MH)
    for k in range(CHUNKS):
        passed_on(T_RX + k, far_source, RX, k * CH, CH, cross)
        passed_on(T_RH + k, RX, RH, k * CH, CH, near)

    block = H * PART
    first_mate = jnp.where(core == 0, 6, 2) * block
    second_mate = jnp.where(core == 0, 2, 6) * block

    def swap(s, part):
        at = (first_mate if part < 2 else second_mate) + (part % 2) * block
        sem = s * 4 + part
        return remote(send.at[s, part], spec.at[s, pl.ds(at, block)], esem.at[sem], fsem.at[sem], mate)

    swaps = {(s, part): swap(s, part) for s in range(SETS) for part in range(4)}

    def give_back(turn, c):
        sem = turn * 2 + c
        return remote(back.at[turn, c], gb.at[turn, c], bsem.at[sem], csem.at[sem], mate)

    def forward(s, o_slot, j_slot, part, begin=0, end=PART // 2):
        first = (part % 2) * PART
        keep = (part % 2 + part // 2 * 4) * block

        def step(i, _):
            a = i * 2
            rho = (orb[o_slot, pl.ds(first + a, 2)] * orb[j_slot, pl.ds(first + a, 2)]).reshape(2 * N, N)
            high, low = split(rho)
            t = mm(jnp.concatenate([high, low], axis=1), wz[...])
            t = t[:, :N] + t[:, N:]
            u = mm(wy[core], stacked(jnp.concatenate([t[:N], t[N:]], axis=1)))
            u = u[:N] + u[N:]
            for b in range(2):
                plane = u[:, b * N : b * N + N]
                spec[s, pl.ds(keep + a + b, H, stride=PART), :] = plane[:H]
                send[s, part, pl.ds(a + b, H, stride=PART), :] = plane[H:]
            return 0

        lax.fori_loop(begin, end, step, 0, unroll=end - begin)
        if end == PART // 2:
            swaps[s, part].start()

    def row_of(s, k):
        return jnp.concatenate(
            [spec[s, pl.ds(pl.multiple_of(p * block + k * PART, PART), PART), :] for p in range(8)], axis=0
        )

    def along_x(s, turn):
        column = row_of(s, 0)
        column = column - jnp.where(zero_mode, jnp.mean(column, axis=0, keepdims=True), 0.0)
        for p in range(8):
            spec[s, pl.ds(p * block, PART), :] = column[p * PART : p * PART + PART]

        def half(c, _):
            def step(i, _):
                k = c * (H // 2) + i * WIDE
                m = jnp.concatenate([row_of(s, k + b) for b in range(WIDE)], axis=1)
                f = mm(wx[...], stacked(m))
                v = jnp.concatenate([vt[pl.ds(pl.multiple_of((k + b) * N, N), N), :] for b in range(WIDE)], axis=1)
                f = (f[:N] + f[N:]) * v
                r = mm(wxi[core], stacked(f))
                r = r[:H] + r[H:]
                for b in range(WIDE):
                    plane = r[:, b * N : b * N + N]
                    ga[turn, c, pl.ds(i * WIDE + b, Q, stride=H // 2), :] = plane[:Q]
                    back[turn, c, pl.ds(i * WIDE + b, Q, stride=H // 2), :] = plane[Q:]
                return 0

            lax.fori_loop(0, H // 2 // WIDE, step, 0, unroll=2)
            give_back(turn, c).start()
            return 0

        lax.fori_loop(0, 2, half, 0)

    def inverse(j_slot, turn, first=False, last=False, parts=(0, 1)):
        if 0 in parts:
            give_back(turn, 0).wait()
            give_back(turn, 1).wait()

        def step(i, _):
            a = i * 2
            planes = []
            for b in range(2):
                rows = pl.ds(pl.multiple_of((a + b) * (H // 2), H // 2), H // 2)
                planes.append(
                    jnp.concatenate([ga[turn, 0, rows, :], ga[turn, 1, rows, :], gb[turn, 0, rows, :], gb[turn, 1, rows, :]], axis=0)
                )
            t = mm(wyi[core], stacked(jnp.concatenate(planes, axis=1)))
            t = t[:N] + t[N:]
            high, low = split(jnp.concatenate([t[:, :N], t[:, N:]], axis=0))
            w = mm(jnp.concatenate([high, low], axis=1), wz[...])
            w = (w[:, :N] + w[:, N:]).reshape(2, N, N) * orb[j_slot, pl.ds(a, 2)]
            if first:
                acc[pl.ds(a, 2)] = w
            else:
                acc[pl.ds(a, 2)] += w
            return 0

        stores = []
        for part in parts:
            lax.fori_loop(part * PART // 2, (part + 1) * PART // 2, step, 0, unroll=UNROLL)
            if last:
                rows = pl.ds(part * PART, PART)
                stores.append(pltpu.make_async_copy(acc.at[rows], out_ref.at[0, rows], lsem.at[part]))
                stores[part].start()
        for store in stores:
            store.wait()

    def spectrum(s, turn):
        for part in (2, 3, 0, 1):
            swaps[s, part].wait()
        along_x(s, turn)

    def arrived(*indices):
        for t in indices:
            moves[t].wait_recv()

    def start(*indices):
        for t in indices:
            moves[t].start()

    def pass_on(*chunks):
        for k in chunks:
            arrived(T_RX + k)
            start(T_RH + k)

    start(T_OXA, T_PXA, T_MHA, T_QHA, T_OXB, T_PXB, T_MHB, T_QHB)
    for fetch in fetches:
        fetch.start()

    strength = N * math.sqrt(N) / 16.0 / float(N**3)
    row = lax.broadcasted_iota(jnp.int32, (N, N), 0)
    column = lax.broadcasted_iota(jnp.int32, (N, N), 1)
    row = jnp.minimum(row, N - row)
    column = jnp.minimum(column, N - column)
    plane = row * row + column * column
    zero_mode = jnp.logical_and(lax.broadcasted_iota(jnp.int32, (1, N), 1) == 0, core == 0)

    def table(i, _):
        ky = core * H + i
        ky = jnp.minimum(ky, N - ky)
        d = (plane + ky * ky).astype(F32)
        vt[pl.ds(pl.multiple_of(i * N, N), N), :] = jnp.where(d > 0, strength / jnp.maximum(d, 1.0), 0.0)
        return 0

    lax.fori_loop(0, H, table, 0)
    for fetch in fetches:
        fetch.wait()
    forward(0, OH, OH, 0)
    forward(0, OH, OH, 1)

    arrived(T_OXA)
    start(T_MXA, T_QXA)
    arrived(T_PXA)
    start(T_PHA)
    arrived(T_MHA, T_QHA)
    start(*range(T_RX, T_RX + EARLY))
    forward(0, OX, OX, 2)
    forward(1, OH, MH, 0)
    forward(2, OH, QH, 0)
    arrived(T_PXB)
    start(T_PHC)
    arrived(T_OXB)
    start(T_MXB, T_QXB, T_PHB)
    arrived(T_MHB, T_QHB)
    start(*range(T_RX + EARLY, T_RX + CHUNKS))
    start(T_RXZ)
    forward(0, OX, OX, 3)
    forward(1, OH, MH, 1)
    forward(2, OH, QH, 1)
    spectrum(0, 0)
    pass_on(0, 1)
    inverse(OH, 0, first=True)
    pass_on(2, 3)
    forward(0, OX, PX, 2)
    forward(0, OX, PX, 3)
    arrived(T_MXA)
    forward(1, OX, MX, 2)
    arrived(T_QXA)
    forward(2, OX, QX, 2)
    arrived(T_PHA)
    forward(0, OH, PH, 0)
    arrived(T_PHC, T_PHB)
    start(T_RHZ)
    forward(0, OH, PH, 1)
    spectrum(0, 1)
    pass_on(4)
    inverse(PH, 1)
    pass_on(5, 6, 7)
    forward(0, OX, RX, 2)
    arrived(T_MXB)
    forward(1, OX, MX, 3)
    pass_on(8)
    arrived(T_QXB)
    forward(2, OX, QX, 3)
    spectrum(1, 0)
    pass_on(9)
    spectrum(2, 1)
    pass_on(10)
    inverse(MH, 0)
    pass_on(11)
    arrived(*range(T_RH, T_RH + 8))
    forward(0, OH, RH, 0)
    pass_on(12)
    over_z = (ZROWS - PART) // 2
    forward(0, OX, RX, 3, end=over_z)
    arrived(T_RXZ)
    forward(0, OX, RX, 3, begin=over_z)
    arrived(*range(T_RH + 8, T_RH + CHUNKS))
    forward(0, OH, RH, 1, end=over_z)
    arrived(T_RHZ)
    forward(0, OH, RH, 1, begin=over_z)
    inverse(QH, 1, parts=(0,))
    spectrum(0, 0)
    inverse(QH, 1, parts=(1,))
    inverse(RH, 0, last=True)
    for t in range(T_COUNT):
        moves[t].wait_send()


def halves(matrix):
    high = matrix.astype(ml_dtypes.bfloat16)
    low = (matrix - high.astype(np.float64)).astype(ml_dtypes.bfloat16)
    return high, low


def left_weight(matrix):
    high, low = halves(matrix)
    return np.concatenate(
        [np.concatenate([high, high], axis=1), np.concatenate([low, np.zeros_like(low)], axis=1)], axis=0
    )


def tables():
    index = np.arange(N)
    angle = 2.0 * np.pi / N * (index[:, None] * index[None, :] % N)
    cas = np.cos(angle) + np.sin(angle)
    high, low = halves(cas)
    wz = np.concatenate(
        [np.concatenate([high, low], axis=1), np.concatenate([high, np.zeros_like(low)], axis=1)], axis=0
    )
    order = [np.concatenate([index[c * H : c * H + H], index[H - c * H : N - c * H]]) for c in (0, 1)]
    wy = np.stack([left_weight(cas[order[c]]) for c in (0, 1)])
    wyi = np.stack([left_weight(cas[:, order[c]]) for c in (0, 1)])
    wx = left_weight(cas)
    kept = [np.concatenate([index[:Q], index[Q : 2 * Q]]), np.concatenate([index[:Q], index[3 * Q :]])]
    wxi = np.stack([left_weight(cas[kept[c]]) for c in (0, 1)])
    return wz, wy, wx, wxi, wyi


def on_device(orbitals):
    weights = [jnp.asarray(w) for w in tables()]
    total = pl.pallas_call(
        kernel,
        out_shape=pltpu.VMEM(orbitals.shape, F32),
        in_specs=[pl.BlockSpec(memory_space=pl.ANY)] * 6,
        out_specs=pl.BlockSpec(memory_space=pl.ANY),
        scratch_shapes=[
            pltpu.VMEM((10, Q, N, N), F32),
            pltpu.VMEM((SETS, N * H, N), F32),
            pltpu.VMEM((SETS, 4, H * PART, N), F32),
            pltpu.VMEM((2, 2, Q * H // 2, N), F32),
            pltpu.VMEM((2, 2, Q * H // 2, N), F32),
            pltpu.VMEM((2, 2, Q * H // 2, N), F32),
            pltpu.VMEM((H * N, N), F32),
            pltpu.VMEM((Q, N, N), F32),
        ]
        + [pltpu.VMEM(w.shape, BF16) for w in weights]
        + [pltpu.SemaphoreType.DMA((n,)) for n in (T_COUNT, T_COUNT, SETS * 4, SETS * 4, 4, 4, 6)],
        compiler_params=pltpu.CompilerParams(
            collective_id=0, has_side_effects=True, vmem_limit_bytes=60 * 1024 * 1024
        ),
    )(orbitals, *weights)
    return -total


def solution(mesh):
    spec = P("band", "grid", None, None)
    return jax.shard_map(on_device, mesh=mesh, in_specs=(spec,), out_specs=spec, check_vma=False)
```

```python
import functools
import math

import jax
import jax.numpy as jnp
import ml_dtypes
import numpy as np
from jax import lax
from jax.experimental import pallas as pl
from jax.experimental.pallas import tpu as pltpu
from jax.sharding import PartitionSpec as P

MESH = pl.DeviceIdType.MESH
BF16 = jnp.bfloat16
F32 = jnp.float32
N = 128
Q = 32
H = 64

OH, OX, PH, PX, MH, MX, QH, QX, RH, RX = range(10)
PART = 16
CH = 2
CHUNKS = 13
ZROWS = CHUNKS * CH
EARLY = 4
(
    T_OXA, T_OXB, T_PXA, T_PXB, T_MHA, T_MHB, T_QHA, T_QHB,
    T_MXA, T_MXB, T_QXA, T_QXB, T_PHA, T_PHB, T_PHC, T_RXZ, T_RHZ,
) = range(17)
T_RX = 17
T_RH = T_RX + CHUNKS
T_COUNT = T_RH + CHUNKS
NEAR_ROWS = 18
SETS = 3
UNROLL = 8
WIDE = 16


def split(value):
    high = value.astype(BF16)
    low = (value - high.astype(F32)).astype(BF16)
    return high, low


def mm(a, b):
    return jnp.dot(a, b, preferred_element_type=F32)


def stacked(value):
    high, low = split(value)
    return jnp.concatenate([high, low], axis=0)


def kernel(
    x_ref, wz_in, wy_in, wx_in, wxi_in, wyi_in, out_ref,
    orb, spec, send, ga, gb, back, vt, acc, wz, wy, wx, wxi, wyi,
    ssem, rsem, esem, fsem, bsem, csem, lsem,
):
    band = lax.axis_index("band")
    grid = lax.axis_index("grid")
    bands = lax.axis_size("band")
    core = grid % 2
    side = band % 2
    mate = (band, grid + 1 - 2 * core)
    near = (band, (grid + 2) % 4)
    cross = (band + 1 - 2 * side, (grid + 2) % 4)
    up = ((band + 2) % bands, grid)
    down = ((band + bands - 2) % bands, grid)
    beyond = (jnp.where(side == 0, up[0], down[0]), grid)

    fetches = [(x_ref.at[0], orb.at[OH]), (wz_in, wz), (wy_in, wy), (wx_in, wx), (wxi_in, wxi), (wyi_in, wyi)]
    fetches = [pltpu.make_async_copy(src, dst, lsem.at[i]) for i, (src, dst) in enumerate(fetches)]
    barrier = pltpu.get_barrier_semaphore()
    for other in (mate, near, cross, up, down):
        pl.semaphore_signal(barrier, inc=1, device_id=other, device_id_type=MESH)
    pl.semaphore_wait(barrier, 5)

    def remote(src, dst, send_sem, recv_sem, device):
        return pltpu.make_async_remote_copy(
            src_ref=src, dst_ref=dst, send_sem=send_sem, recv_sem=recv_sem, device_id=device, device_id_type=MESH
        )

    moves = {}

    def transfer(index, src, dst, device):
        moves[index] = remote(src, dst, ssem.at[index], rsem.at[index], device)

    def passed_on(index, src_slot, dst_slot, first, count, device):
        rows = pl.ds(first, count)
        transfer(index, orb.at[src_slot, rows], orb.at[dst_slot, rows], device)

    for index, slot, device in ((T_OXA, OX, near), (T_PXA, PX, cross), (T_MHA, MH, up), (T_QHA, QH, down)):
        for part in range(2):
            rows = pl.ds(part * PART, PART)
            transfer(index + part, x_ref.at[0, rows], orb.at[slot, rows], device)
    passed_on(T_MXA, OX, MX, 0, PART, up)
    passed_on(T_MXB, OX, MX, PART, PART, up)
    passed_on(T_QXA, OX, QX, 0, PART, down)
    passed_on(T_QXB, OX, QX, PART, PART, down)
    passed_on(T_PHA, PX, PH, 0, PART, near)
    passed_on(T_PHC, PX, PH, PART, NEAR_ROWS - PART, near)
    passed_on(T_PHB, OX, PH, NEAR_ROWS, Q - NEAR_ROWS, cross)
    passed_on(T_RXZ, PX, RX, ZROWS, Q - ZROWS, beyond)
    passed_on(T_RHZ, PH, RH, ZROWS, Q - ZROWS, beyond)
    far_source = jnp.where(side == 0, QH, MH)
    for k in range(CHUNKS):
        passed_on(T_RX + k, far_source, RX, k * CH, CH, cross)
        passed_on(T_RH + k, RX, RH, k * CH, CH, near)

    block = H * PART
    first_mate = jnp.where(core == 0, 6, 2) * block
    second_mate = jnp.where(core == 0, 2, 6) * block

    def swap(s, part):
        at = (first_mate if part < 2 else second_mate) + (part % 2) * block
        sem = s * 4 + part
        return remote(send.at[s, part], spec.at[s, pl.ds(at, block)], esem.at[sem], fsem.at[sem], mate)

    swaps = {(s, part): swap(s, part) for s in range(SETS) for part in range(4)}

    def give_back(turn, c):
        sem = turn * 2 + c
        return remote(back.at[turn, c], gb.at[turn, c], bsem.at[sem], csem.at[sem], mate)

    def forward(s, o_slot, j_slot, part, begin=0, end=PART // 2):
        first = (part % 2) * PART
        keep = (part % 2 + part // 2 * 4) * block

        def step(i, _):
            a = i * 2
            rho = (orb[o_slot, pl.ds(first + a, 2)] * orb[j_slot, pl.ds(first + a, 2)]).reshape(2 * N, N)
            high, low = split(rho)
            t = mm(jnp.concatenate([high, low], axis=1), wz[...])
            t = t[:, :N] + t[:, N:]
            u = mm(wy[core], stacked(jnp.concatenate([t[:N], t[N:]], axis=1)))
            u = u[:N] + u[N:]
            for b in range(2):
                plane = u[:, b * N : b * N + N]
                spec[s, pl.ds(keep + a + b, H, stride=PART), :] = plane[:H]
                send[s, part, pl.ds(a + b, H, stride=PART), :] = plane[H:]
            return 0

        lax.fori_loop(begin, end, step, 0, unroll=end - begin)
        if end == PART // 2:
            swaps[s, part].start()

    def row_of(s, k):
        return jnp.concatenate(
            [spec[s, pl.ds(pl.multiple_of(p * block + k * PART, PART), PART), :] for p in range(8)], axis=0
        )

    def along_x(s, turn, chunk):
        column = row_of(s, 0)
        column = column - jnp.where(zero_mode, jnp.mean(column, axis=0, keepdims=True), 0.0)
        for p in range(8):
            spec[s, pl.ds(p * block, PART), :] = column[p * PART : p * PART + PART]

        def half(c, _):
            def step(i, _):
                k = c * (H // 2) + i * WIDE
                m = jnp.concatenate([row_of(s, k + b) for b in range(WIDE)], axis=1)
                f = mm(wx[...], stacked(m))
                v = jnp.concatenate([vt[pl.ds(pl.multiple_of((k + b) * N, N), N), :] for b in range(WIDE)], axis=1)
                f = (f[:N] + f[N:]) * v
                r = mm(wxi[core], stacked(f))
                r = r[:H] + r[H:]
                for b in range(WIDE):
                    plane = r[:, b * N : b * N + N]
                    ga[turn, c, pl.ds(i * WIDE + b, Q, stride=H // 2), :] = plane[:Q]
                    back[turn, c, pl.ds(i * WIDE + b, Q, stride=H // 2), :] = plane[Q:]
                return 0

            lax.fori_loop(0, H // 2 // WIDE, step, 0, unroll=2)
            give_back(turn, c).start()
            if chunk is not None:

                @pl.when(c == 0)
                def _():
                    pass_on(chunk)

            return 0

        lax.fori_loop(0, 2, half, 0)

    def inverse(j_slot, turn, first=False, last=False, parts=(0, 1)):
        if 0 in parts:
            give_back(turn, 0).wait()
            give_back(turn, 1).wait()

        def step(i, _):
            a = i * 2
            planes = []
            for b in range(2):
                rows = pl.ds(pl.multiple_of((a + b) * (H // 2), H // 2), H // 2)
                planes.append(
                    jnp.concatenate([ga[turn, 0, rows, :], ga[turn, 1, rows, :], gb[turn, 0, rows, :], gb[turn, 1, rows, :]], axis=0)
                )
            t = mm(wyi[core], stacked(jnp.concatenate(planes, axis=1)))
            t = t[:N] + t[N:]
            high, low = split(jnp.concatenate([t[:, :N], t[:, N:]], axis=0))
            w = mm(jnp.concatenate([high, low], axis=1), wz[...])
            w = (w[:, :N] + w[:, N:]).reshape(2, N, N) * orb[j_slot, pl.ds(a, 2)]
            if first:
                acc[pl.ds(a, 2)] = w
            else:
                acc[pl.ds(a, 2)] += w
            return 0

        stores = []
        for part in parts:
            lax.fori_loop(part * PART // 2, (part + 1) * PART // 2, step, 0, unroll=UNROLL)
            if last:
                rows = pl.ds(part * PART, PART)
                stores.append(pltpu.make_async_copy(acc.at[rows], out_ref.at[0, rows], lsem.at[part]))
                stores[part].start()
        for store in stores:
            store.wait()

    def spectrum(s, turn, chunk=None):
        for part in (2, 3, 0, 1):
            swaps[s, part].wait()
        along_x(s, turn, chunk)

    def arrived(*indices):
        for t in indices:
            moves[t].wait_recv()

    def start(*indices):
        for t in indices:
            moves[t].start()

    def pass_on(*chunks):
        for k in chunks:
            arrived(T_RX + k)
            start(T_RH + k)

    start(T_OXA, T_PXA, T_MHA, T_QHA, T_OXB, T_PXB, T_MHB, T_QHB)
    for fetch in fetches:
        fetch.start()

    strength = N * math.sqrt(N) / 16.0 / float(N**3)
    row = lax.broadcasted_iota(jnp.int32, (N, N), 0)
    column = lax.broadcasted_iota(jnp.int32, (N, N), 1)
    row = jnp.minimum(row, N - row)
    column = jnp.minimum(column, N - column)
    plane = row * row + column * column
    zero_mode = jnp.logical_and(lax.broadcasted_iota(jnp.int32, (1, N), 1) == 0, core == 0)

    def table(i, _):
        ky = core * H + i
        ky = jnp.minimum(ky, N - ky)
        d = (plane + ky * ky).astype(F32)
        vt[pl.ds(pl.multiple_of(i * N, N), N), :] = jnp.where(d > 0, strength / jnp.maximum(d, 1.0), 0.0)
        return 0

    lax.fori_loop(0, H, table, 0)
    for fetch in fetches:
        fetch.wait()
    forward(0, OH, OH, 0)
    forward(0, OH, OH, 1)

    arrived(T_OXA)
    start(T_MXA, T_QXA)
    arrived(T_PXA)
    start(T_PHA)
    arrived(T_MHA, T_QHA)
    start(*range(T_RX, T_RX + EARLY))
    forward(0, OX, OX, 2)
    forward(1, OH, MH, 0)
    forward(2, OH, QH, 0)
    arrived(T_PXB)
    start(T_PHC)
    arrived(T_OXB)
    start(T_MXB, T_QXB, T_PHB)
    arrived(T_MHB, T_QHB)
    start(*range(T_RX + EARLY, T_RX + CHUNKS))
    start(T_RXZ)
    forward(0, OX, OX, 3)
    forward(1, OH, MH, 1)
    forward(2, OH, QH, 1)
    spectrum(0, 0)
    pass_on(0, 1)
    inverse(OH, 0, first=True)
    pass_on(2, 3)
    forward(0, OX, PX, 2)
    forward(0, OX, PX, 3)
    arrived(T_MXA)
    forward(1, OX, MX, 2)
    arrived(T_QXA)
    forward(2, OX, QX, 2)
    arrived(T_PHA)
    forward(0, OH, PH, 0)
    arrived(T_PHC, T_PHB)
    start(T_RHZ)
    forward(0, OH, PH, 1)
    spectrum(0, 1, chunk=4)
    inverse(PH, 1, parts=(0,))
    pass_on(5)
    inverse(PH, 1, parts=(1,))
    pass_on(6, 7)
    forward(0, OX, RX, 2)
    arrived(T_MXB)
    forward(1, OX, MX, 3)
    pass_on(8)
    arrived(T_QXB)
    forward(2, OX, QX, 3)
    spectrum(1, 0, chunk=9)
    spectrum(2, 1, chunk=10)
    inverse(MH, 0, parts=(0,))
    pass_on(11)
    inverse(MH, 0, parts=(1,))
    arrived(*range(T_RH, T_RH + 8))
    forward(0, OH, RH, 0)
    pass_on(12)
    over_z = (ZROWS - PART) // 2
    forward(0, OX, RX, 3, end=over_z)
    arrived(T_RXZ)
    forward(0, OX, RX, 3, begin=over_z)
    arrived(*range(T_RH + 8, T_RH + CHUNKS))
    forward(0, OH, RH, 1, end=over_z)
    arrived(T_RHZ)
    forward(0, OH, RH, 1, begin=over_z)
    inverse(QH, 1, parts=(0,))
    spectrum(0, 0)
    inverse(QH, 1, parts=(1,))
    inverse(RH, 0, last=True)
    for t in range(T_COUNT):
        moves[t].wait_send()


def halves(matrix):
    high = matrix.astype(ml_dtypes.bfloat16)
    low = (matrix - high.astype(np.float64)).astype(ml_dtypes.bfloat16)
    return high, low


def left_weight(matrix):
    high, low = halves(matrix)
    return np.concatenate(
        [np.concatenate([high, high], axis=1), np.concatenate([low, np.zeros_like(low)], axis=1)], axis=0
    )


def tables():
    index = np.arange(N)
    angle = 2.0 * np.pi / N * (index[:, None] * index[None, :] % N)
    cas = np.cos(angle) + np.sin(angle)
    high, low = halves(cas)
    wz = np.concatenate(
        [np.concatenate([high, low], axis=1), np.concatenate([high, np.zeros_like(low)], axis=1)], axis=0
    )
    order = [np.concatenate([index[c * H : c * H + H], index[H - c * H : N - c * H]]) for c in (0, 1)]
    wy = np.stack([left_weight(cas[order[c]]) for c in (0, 1)])
    wyi = np.stack([left_weight(cas[:, order[c]]) for c in (0, 1)])
    wx = left_weight(cas)
    kept = [np.concatenate([index[:Q], index[Q : 2 * Q]]), np.concatenate([index[:Q], index[3 * Q :]])]
    wxi = np.stack([left_weight(cas[kept[c]]) for c in (0, 1)])
    return wz, wy, wx, wxi, wyi


def on_device(orbitals):
    weights = [jnp.asarray(w) for w in tables()]
    total = pl.pallas_call(
        kernel,
        out_shape=pltpu.VMEM(orbitals.shape, F32),
        in_specs=[pl.BlockSpec(memory_space=pl.ANY)] * 6,
        out_specs=pl.BlockSpec(memory_space=pl.ANY),
        scratch_shapes=[
            pltpu.VMEM((10, Q, N, N), F32),
            pltpu.VMEM((SETS, N * H, N), F32),
            pltpu.VMEM((SETS, 4, H * PART, N), F32),
            pltpu.VMEM((2, 2, Q * H // 2, N), F32),
            pltpu.VMEM((2, 2, Q * H // 2, N), F32),
            pltpu.VMEM((2, 2, Q * H // 2, N), F32),
            pltpu.VMEM((H * N, N), F32),
            pltpu.VMEM((Q, N, N), F32),
        ]
        + [pltpu.VMEM(w.shape, BF16) for w in weights]
        + [pltpu.SemaphoreType.DMA((n,)) for n in (T_COUNT, T_COUNT, SETS * 4, SETS * 4, 4, 4, 6)],
        compiler_params=pltpu.CompilerParams(
            collective_id=0, has_side_effects=True, vmem_limit_bytes=60 * 1024 * 1024
        ),
    )(orbitals, *weights)
    return -total


def solution(mesh):
    spec = P("band", "grid", None, None)
    return jax.shard_map(on_device, mesh=mesh, in_specs=(spec,), out_specs=spec, check_vma=False)
```

```python
import functools
import math

import jax
import jax.numpy as jnp
import ml_dtypes
import numpy as np
from jax import lax
from jax.experimental import pallas as pl
from jax.experimental.pallas import tpu as pltpu
from jax.sharding import PartitionSpec as P

MESH = pl.DeviceIdType.MESH
BF16 = jnp.bfloat16
F32 = jnp.float32
N = 128
Q = 32
H = 64

OH, OX, PH, PX, MH, MX, QH, QX, RH, RX = range(10)
PART = 16
CH = 2
CHUNKS = 13
ZROWS = CHUNKS * CH
EARLY = 4
(
    T_OXA, T_OXB, T_PXA, T_PXB, T_MHA, T_MHB, T_QHA, T_QHB,
    T_MXA, T_MXB, T_QXA, T_QXB, T_PHA, T_PHB, T_PHC, T_RXZ, T_RHZ,
) = range(17)
T_RX = 17
T_RH = T_RX + CHUNKS
T_COUNT = T_RH + CHUNKS
NEAR_ROWS = 17
SETS = 3
UNROLL = 8
WIDE = 16


def split(value):
    high = value.astype(BF16)
    low = (value - high.astype(F32)).astype(BF16)
    return high, low


def mm(a, b):
    return jnp.dot(a, b, preferred_element_type=F32)


def stacked(value):
    high, low = split(value)
    return jnp.concatenate([high, low], axis=0)


def kernel(
    x_ref, wz_in, wy_in, wx_in, wxi_in, wyi_in, out_ref,
    orb, spec, send, ga, gb, back, vt, acc, wz, wy, wx, wxi, wyi,
    ssem, rsem, esem, fsem, bsem, csem, lsem,
):
    band = lax.axis_index("band")
    grid = lax.axis_index("grid")
    bands = lax.axis_size("band")
    core = grid % 2
    side = band % 2
    mate = (band, grid + 1 - 2 * core)
    near = (band, (grid + 2) % 4)
    cross = (band + 1 - 2 * side, (grid + 2) % 4)
    up = ((band + 2) % bands, grid)
    down = ((band + bands - 2) % bands, grid)
    beyond = (jnp.where(side == 0, up[0], down[0]), grid)

    fetches = [(x_ref.at[0], orb.at[OH]), (wz_in, wz), (wy_in, wy), (wx_in, wx), (wxi_in, wxi), (wyi_in, wyi)]
    fetches = [pltpu.make_async_copy(src, dst, lsem.at[i]) for i, (src, dst) in enumerate(fetches)]
    barrier = pltpu.get_barrier_semaphore()
    for other in (mate, near, cross, up, down):
        pl.semaphore_signal(barrier, inc=1, device_id=other, device_id_type=MESH)
    pl.semaphore_wait(barrier, 5)

    def remote(src, dst, send_sem, recv_sem, device):
        return pltpu.make_async_remote_copy(
            src_ref=src, dst_ref=dst, send_sem=send_sem, recv_sem=recv_sem, device_id=device, device_id_type=MESH
        )

    moves = {}

    def transfer(index, src, dst, device):
        moves[index] = remote(src, dst, ssem.at[index], rsem.at[index], device)

    def passed_on(index, src_slot, dst_slot, first, count, device):
        rows = pl.ds(first, count)
        transfer(index, orb.at[src_slot, rows], orb.at[dst_slot, rows], device)

    for index, slot, device in ((T_OXA, OX, near), (T_PXA, PX, cross), (T_MHA, MH, up), (T_QHA, QH, down)):
        for part in range(2):
            rows = pl.ds(part * PART, PART)
            transfer(index + part, x_ref.at[0, rows], orb.at[slot, rows], device)
    passed_on(T_MXA, OX, MX, 0, PART, up)
    passed_on(T_MXB, OX, MX, PART, PART, up)
    passed_on(T_QXA, OX, QX, 0, PART, down)
    passed_on(T_QXB, OX, QX, PART, PART, down)
    passed_on(T_PHA, PX, PH, 0, PART, near)
    passed_on(T_PHC, PX, PH, PART, NEAR_ROWS - PART, near)
    passed_on(T_PHB, OX, PH, NEAR_ROWS, Q - NEAR_ROWS, cross)
    passed_on(T_RXZ, PX, RX, ZROWS, Q - ZROWS, beyond)
    passed_on(T_RHZ, PH, RH, ZROWS, Q - ZROWS, beyond)
    far_source = jnp.where(side == 0, QH, MH)
    for k in range(CHUNKS):
        passed_on(T_RX + k, far_source, RX, k * CH, CH, cross)
        passed_on(T_RH + k, RX, RH, k * CH, CH, near)

    block = H * PART
    first_mate = jnp.where(core == 0, 6, 2) * block
    second_mate = jnp.where(core == 0, 2, 6) * block

    def swap(s, part):
        at = (first_mate if part < 2 else second_mate) + (part % 2) * block
        sem = s * 4 + part
        return remote(send.at[s, part], spec.at[s, pl.ds(at, block)], esem.at[sem], fsem.at[sem], mate)

    swaps = {(s, part): swap(s, part) for s in range(SETS) for part in range(4)}

    def give_back(turn, c):
        sem = turn * 2 + c
        return remote(back.at[turn, c], gb.at[turn, c], bsem.at[sem], csem.at[sem], mate)

    def forward(s, o_slot, j_slot, part, begin=0, end=PART // 2):
        first = (part % 2) * PART
        keep = (part % 2 + part // 2 * 4) * block

        def step(i, _):
            a = i * 2
            rho = (orb[o_slot, pl.ds(first + a, 2)] * orb[j_slot, pl.ds(first + a, 2)]).reshape(2 * N, N)
            high, low = split(rho)
            t = mm(jnp.concatenate([high, low], axis=1), wz[...])
            t = t[:, :N] + t[:, N:]
            u = mm(wy[core], stacked(jnp.concatenate([t[:N], t[N:]], axis=1)))
            u = u[:N] + u[N:]
            for b in range(2):
                plane = u[:, b * N : b * N + N]
                spec[s, pl.ds(keep + a + b, H, stride=PART), :] = plane[:H]
                send[s, part, pl.ds(a + b, H, stride=PART), :] = plane[H:]
            return 0

        lax.fori_loop(begin, end, step, 0, unroll=end - begin)
        if end == PART // 2:
            swaps[s, part].start()

    def row_of(s, k):
        return jnp.concatenate(
            [spec[s, pl.ds(pl.multiple_of(p * block + k * PART, PART), PART), :] for p in range(8)], axis=0
        )

    def along_x(s, turn, chunk):
        column = row_of(s, 0)
        column = column - jnp.where(zero_mode, jnp.mean(column, axis=0, keepdims=True), 0.0)
        for p in range(8):
            spec[s, pl.ds(p * block, PART), :] = column[p * PART : p * PART + PART]

        def half(c, _):
            def step(i, _):
                k = c * (H // 2) + i * WIDE
                m = jnp.concatenate([row_of(s, k + b) for b in range(WIDE)], axis=1)
                f = mm(wx[...], stacked(m))
                v = jnp.concatenate([vt[pl.ds(pl.multiple_of((k + b) * N, N), N), :] for b in range(WIDE)], axis=1)
                f = (f[:N] + f[N:]) * v
                r = mm(wxi[core], stacked(f))
                r = r[:H] + r[H:]
                for b in range(WIDE):
                    plane = r[:, b * N : b * N + N]
                    ga[turn, c, pl.ds(i * WIDE + b, Q, stride=H // 2), :] = plane[:Q]
                    back[turn, c, pl.ds(i * WIDE + b, Q, stride=H // 2), :] = plane[Q:]
                return 0

            lax.fori_loop(0, H // 2 // WIDE, step, 0, unroll=2)
            give_back(turn, c).start()
            if chunk is not None:

                @pl.when(c == 0)
                def _():
                    pass_on(chunk)

            return 0

        lax.fori_loop(0, 2, half, 0)

    def inverse(j_slot, turn, first=False, last=False, parts=(0, 1)):
        if 0 in parts:
            give_back(turn, 0).wait()
            give_back(turn, 1).wait()

        def step(i, _):
            a = i * 2
            planes = []
            for b in range(2):
                rows = pl.ds(pl.multiple_of((a + b) * (H // 2), H // 2), H // 2)
                planes.append(
                    jnp.concatenate([ga[turn, 0, rows, :], ga[turn, 1, rows, :], gb[turn, 0, rows, :], gb[turn, 1, rows, :]], axis=0)
                )
            t = mm(wyi[core], stacked(jnp.concatenate(planes, axis=1)))
            t = t[:N] + t[N:]
            high, low = split(jnp.concatenate([t[:, :N], t[:, N:]], axis=0))
            w = mm(jnp.concatenate([high, low], axis=1), wz[...])
            w = (w[:, :N] + w[:, N:]).reshape(2, N, N) * orb[j_slot, pl.ds(a, 2)]
            if first:
                acc[pl.ds(a, 2)] = w
            else:
                acc[pl.ds(a, 2)] += w
            return 0

        stores = []
        for part in parts:
            lax.fori_loop(part * PART // 2, (part + 1) * PART // 2, step, 0, unroll=UNROLL)
            if last:
                rows = pl.ds(part * PART, PART)
                stores.append(pltpu.make_async_copy(acc.at[rows], out_ref.at[0, rows], lsem.at[part]))
                stores[part].start()
        for store in stores:
            store.wait()

    def spectrum(s, turn, chunk=None):
        for part in (2, 3, 0, 1):
            swaps[s, part].wait()
        along_x(s, turn, chunk)

    def arrived(*indices):
        for t in indices:
            moves[t].wait_recv()

    def start(*indices):
        for t in indices:
            moves[t].start()

    def pass_on(*chunks):
        for k in chunks:
            arrived(T_RX + k)
            start(T_RH + k)

    start(T_OXA, T_PXA, T_MHA, T_QHA, T_OXB, T_PXB, T_MHB, T_QHB)
    for fetch in fetches:
        fetch.start()

    strength = N * math.sqrt(N) / 16.0 / float(N**3)
    row = lax.broadcasted_iota(jnp.int32, (N, N), 0)
    column = lax.broadcasted_iota(jnp.int32, (N, N), 1)
    row = jnp.minimum(row, N - row)
    column = jnp.minimum(column, N - column)
    plane = row * row + column * column
    zero_mode = jnp.logical_and(lax.broadcasted_iota(jnp.int32, (1, N), 1) == 0, core == 0)

    def table(i, _):
        ky = core * H + i
        ky = jnp.minimum(ky, N - ky)
        d = (plane + ky * ky).astype(F32)
        vt[pl.ds(pl.multiple_of(i * N, N), N), :] = jnp.where(d > 0, strength / jnp.maximum(d, 1.0), 0.0)
        return 0

    lax.fori_loop(0, H, table, 0)
    for fetch in fetches:
        fetch.wait()
    forward(0, OH, OH, 0)
    forward(0, OH, OH, 1)

    arrived(T_OXA)
    start(T_MXA, T_QXA)
    arrived(T_PXA)
    start(T_PHA)
    arrived(T_MHA, T_QHA)
    start(*range(T_RX, T_RX + EARLY))
    forward(0, OX, OX, 2)
    forward(1, OH, MH, 0)
    forward(2, OH, QH, 0)
    arrived(T_PXB)
    start(T_PHC)
    arrived(T_OXB)
    start(T_MXB, T_QXB, T_PHB)
    arrived(T_MHB, T_QHB)
    start(*range(T_RX + EARLY, T_RX + CHUNKS))
    start(T_RXZ)
    forward(0, OX, OX, 3)
    forward(1, OH, MH, 1)
    forward(2, OH, QH, 1)
    spectrum(0, 0)
    pass_on(0, 1)
    inverse(OH, 0, first=True)
    pass_on(2, 3)
    forward(0, OX, PX, 2)
    forward(0, OX, PX, 3)
    arrived(T_MXA)
    forward(1, OX, MX, 2)
    arrived(T_QXA)
    forward(2, OX, QX, 2)
    arrived(T_PHA)
    forward(0, OH, PH, 0)
    arrived(T_PHC, T_PHB)
    start(T_RHZ)
    forward(0, OH, PH, 1)
    spectrum(0, 1, chunk=4)
    inverse(PH, 1, parts=(0,))
    pass_on(5)
    inverse(PH, 1, parts=(1,))
    pass_on(6, 7)
    forward(0, OX, RX, 2)
    arrived(T_MXB)
    forward(1, OX, MX, 3)
    pass_on(8)
    arrived(T_QXB)
    forward(2, OX, QX, 3)
    spectrum(1, 0, chunk=9)
    spectrum(2, 1, chunk=10)
    inverse(MH, 0, parts=(0,))
    pass_on(11)
    inverse(MH, 0, parts=(1,))
    arrived(*range(T_RH, T_RH + 8))
    forward(0, OH, RH, 0)
    pass_on(12)
    over_z = (ZROWS - PART) // 2
    forward(0, OX, RX, 3, end=over_z)
    arrived(T_RXZ)
    forward(0, OX, RX, 3, begin=over_z)
    arrived(*range(T_RH + 8, T_RH + CHUNKS))
    forward(0, OH, RH, 1, end=over_z)
    arrived(T_RHZ)
    forward(0, OH, RH, 1, begin=over_z)
    inverse(QH, 1, parts=(0,))
    spectrum(0, 0)
    inverse(QH, 1, parts=(1,))
    inverse(RH, 0, last=True)
    for t in range(T_COUNT):
        moves[t].wait_send()


def halves(matrix):
    high = matrix.astype(ml_dtypes.bfloat16)
    low = (matrix - high.astype(np.float64)).astype(ml_dtypes.bfloat16)
    return high, low


def left_weight(matrix):
    high, low = halves(matrix)
    return np.concatenate(
        [np.concatenate([high, high], axis=1), np.concatenate([low, np.zeros_like(low)], axis=1)], axis=0
    )


def tables():
    index = np.arange(N)
    angle = 2.0 * np.pi / N * (index[:, None] * index[None, :] % N)
    cas = np.cos(angle) + np.sin(angle)
    high, low = halves(cas)
    wz = np.concatenate(
        [np.concatenate([high, low], axis=1), np.concatenate([high, np.zeros_like(low)], axis=1)], axis=0
    )
    order = [np.concatenate([index[c * H : c * H + H], index[H - c * H : N - c * H]]) for c in (0, 1)]
    wy = np.stack([left_weight(cas[order[c]]) for c in (0, 1)])
    wyi = np.stack([left_weight(cas[:, order[c]]) for c in (0, 1)])
    wx = left_weight(cas)
    kept = [np.concatenate([index[:Q], index[Q : 2 * Q]]), np.concatenate([index[:Q], index[3 * Q :]])]
    wxi = np.stack([left_weight(cas[kept[c]]) for c in (0, 1)])
    return wz, wy, wx, wxi, wyi


def on_device(orbitals):
    weights = [jnp.asarray(w) for w in tables()]
    total = pl.pallas_call(
        kernel,
        out_shape=pltpu.VMEM(orbitals.shape, F32),
        in_specs=[pl.BlockSpec(memory_space=pl.ANY)] * 6,
        out_specs=pl.BlockSpec(memory_space=pl.ANY),
        scratch_shapes=[
            pltpu.VMEM((10, Q, N, N), F32),
            pltpu.VMEM((SETS, N * H, N), F32),
            pltpu.VMEM((SETS, 4, H * PART, N), F32),
            pltpu.VMEM((2, 2, Q * H // 2, N), F32),
            pltpu.VMEM((2, 2, Q * H // 2, N), F32),
            pltpu.VMEM((2, 2, Q * H // 2, N), F32),
            pltpu.VMEM((H * N, N), F32),
            pltpu.VMEM((Q, N, N), F32),
        ]
        + [pltpu.VMEM(w.shape, BF16) for w in weights]
        + [pltpu.SemaphoreType.DMA((n,)) for n in (T_COUNT, T_COUNT, SETS * 4, SETS * 4, 4, 4, 6)],
        compiler_params=pltpu.CompilerParams(
            collective_id=0, has_side_effects=True, vmem_limit_bytes=60 * 1024 * 1024
        ),
    )(orbitals, *weights)
    return -total


def solution(mesh):
    spec = P("band", "grid", None, None)
    return jax.shard_map(on_device, mesh=mesh, in_specs=(spec,), out_specs=spec, check_vma=False)
```
